512 devices in a mesh: fsdp: 8 (over y_hi, core), replica: 64 (over y_lo, x, z).
Axes of the slice: x: 4, y: 8 (y_hi: 4, y_lo: 2; y = y_hi * 2 + y_lo), z: 8, core: 2. Of those that a mesh axis runs over, the one named last changes fastest.
Arguments:
- tokens: bfloat16 [64, 1024, 4096], P('replica', 'fsdp'), may hold values from -6 to 6
- cotangent: bfloat16 [64, 1024, 4096], P('replica', 'fsdp'), may hold values from -0.1796875 to 0.1796875
- w_gate: bfloat16 [4096, 256], P('fsdp'), may hold values from -0.09375 to 0.09375
- w_up: bfloat16 [4096, 256], P('fsdp'), may hold values from -0.09375 to 0.09375
- w_down: bfloat16 [256, 4096], P(None, 'fsdp'), may hold values from -0.375 to 0.375
- delta: float32 [64, 128, 4096], P('replica', 'fsdp'), may hold values from -6 to 6
- anchor: float32 [128, 4096], P('fsdp'), may hold values from -3 to 3
- momentum: float32 [128, 4096], P('fsdp'), may hold values from -1.8 to 1.8
Outputs:
- grad_gate: bfloat16 [64, 4096, 256], P('replica', 'fsdp')
- grad_up: bfloat16 [64, 4096, 256], P('replica', 'fsdp')
- grad_down: bfloat16 [64, 256, 4096], P('replica', None, 'fsdp')
- new_anchor: float32 [128, 4096], P('fsdp')
- new_momentum: float32 [128, 4096], P('fsdp')
The draws below stay inside these ranges and needn't reach their ends.
All inputs are finite; a program needn't handle non-finite values.
Results may differ from the reference program's by a relative error of at most 0.0049.
Values may be sent and summed in bfloat16 or wider, within the bound.
No kernel may reach another device: no remote copies, remote signals or barrier semaphores. Data moves between devices by JAX's collectives and lax.ppermute only.
A program may use at most 64 MiB of HBM per device.

```python
import jax
import jax.numpy as jnp
from jax import lax

D = 4096
F = 256
TOKENS = 1024
FRAG = 128
N_REPLICA = 64


def steps_of(stream_key, dims, split, low, high):
    level = 1.0
    for position, shards_of in split:
        steps = jax.random.uniform(jax.random.fold_in(jax.random.fold_in(stream_key, 6), position), (shards_of,), jnp.float32, low / len(split), high / len(split))
        level = level * jnp.repeat(jnp.exp(steps), dims[position] // shards_of).reshape((-1,) + (1,) * (len(dims) - 1 - position))
    return level


def noise(rng, shape, width, most, cuts=(), dtype=jnp.bfloat16):
    array = width * jax.random.normal(rng, shape, jnp.float32)
    if cuts:
        array = array * steps_of(rng, shape, cuts, -0.22, 0.18)
    return jnp.clip(array, -most, most).astype(dtype)


def setup_inputs(seed: int = 0) -> dict:
    splits = jax.random.split(jax.random.key(seed), 9)
    return {
        "tokens": noise(splits[0], (N_REPLICA, TOKENS, D), 1.0, 6.0, ((0, 64), (1, 8))),
        "cotangent": noise(splits[1], (N_REPLICA, TOKENS, D), 0.03, 0.1796875, ((0, 64), (1, 8))),
        "w_gate": noise(splits[2], (D, F), D ** -0.5, 0.09375, ((0, 8),)),
        "w_up": noise(splits[3], (D, F), D ** -0.5, 0.09375, ((0, 8),)),
        "w_down": noise(splits[4], (F, D), F ** -0.5, 0.375, ((1, 8),)),
        "delta": noise(splits[5], (N_REPLICA, FRAG, D), 1.0, 6.0, ((0, 64), (1, 8)), jnp.float32),
        "anchor": noise(splits[6], (FRAG, D), 0.5, 3.0, ((0, 8),), jnp.float32),
        "momentum": noise(splits[7], (FRAG, D), 0.3, 1.8, ((0, 8),), jnp.float32),
    }


def one_replica(x, dy, w_gate, w_up, w_down):
    gate = jnp.dot(x, w_gate, preferred_element_type=jnp.float32)
    up = jnp.dot(x, w_up, preferred_element_type=jnp.float32)
    d_hidden = jnp.dot(dy, w_down.T, preferred_element_type=jnp.float32)
    sig = jax.nn.sigmoid(gate)
    active = gate * sig
    slope = sig * (1.0 + gate * (1.0 - sig))
    hidden = (active * up).astype(jnp.bfloat16)
    d_up = (d_hidden * active).astype(jnp.bfloat16)
    d_gate = (d_hidden * up * slope).astype(jnp.bfloat16)
    grad_gate = jnp.dot(x.T, d_gate, preferred_element_type=jnp.float32).astype(jnp.bfloat16)
    grad_up = jnp.dot(x.T, d_up, preferred_element_type=jnp.float32).astype(jnp.bfloat16)
    grad_down = jnp.dot(hidden.T, dy, preferred_element_type=jnp.float32).astype(jnp.bfloat16)
    return grad_gate, grad_up, grad_down


def reference(tokens, cotangent, w_gate, w_up, w_down, delta, anchor, momentum):
    def step(pair):
        return one_replica(pair[0], pair[1], w_gate, w_up, w_down)

    grad_gate, grad_up, grad_down = lax.map(step, (tokens, cotangent))
    pseudo = jnp.sum(delta, axis=0) / N_REPLICA
    new_momentum = 0.9 * momentum + pseudo
    new_anchor = anchor - 0.7 * (pseudo + 0.9 * new_momentum)
    return grad_gate, grad_up, grad_down, new_anchor, new_momentum
```

```python
import functools

import jax
import jax.numpy as jnp
from jax import lax
from jax.experimental import pallas as pl
from jax.experimental.pallas import tpu as pltpu
from jax.sharding import Mesh
from jax.sharding import PartitionSpec as P

CHIPS = 4
ROWS = 128
WIDE = 1024
HALF = 512
HID = 256
VMEM_LIMIT = 48 * 1024 * 1024

F32 = jnp.float32
BF16 = jnp.bfloat16
ANY = pl.BlockSpec(memory_space=pl.ANY)
VMEM = pl.BlockSpec(memory_space=pltpu.VMEM)
SMEM = pl.BlockSpec(memory_space=pltpu.SMEM)


def run_copies(copies, sems):
    started = [pltpu.make_async_copy(src, dst, sems.at[i]) for i, (src, dst) in enumerate(copies)]
    for copy in started:
        copy.start()
    return started


def columns(base, width):
    return pl.ds(pl.multiple_of(base, HALF), width)


def pack_kernel(place, x, dy, one, two, three, beside, sems):
    chip, core = place[0], place[1]
    copies = []
    for shift in range(CHIPS):
        block = lax.rem(chip + shift, CHIPS) * WIDE
        if shift:
            target = (one, two, three)[shift - 1]
            copies += [(x.at[:, columns(block, WIDE)], target.at[0]), (dy.at[:, columns(block, WIDE)], target.at[1])]
        other = columns(block + (1 - core) * HALF, HALF)
        copies += [(x.at[:, other], beside.at[shift, 0]), (dy.at[:, other], beside.at[shift, 1])]
    for copy in run_copies(copies, sems):
        copy.wait()


def pack(place, x, dy):
    wide = jax.ShapeDtypeStruct((2, ROWS, WIDE), BF16)
    return pl.pallas_call(
        pack_kernel,
        out_shape=(wide, wide, wide, jax.ShapeDtypeStruct((CHIPS, 2, ROWS, HALF), BF16)),
        in_specs=[SMEM, ANY, ANY],
        out_specs=(ANY,) * 4,
        scratch_shapes=[pltpu.SemaphoreType.DMA((14,))],
        cost_estimate=pl.CostEstimate(flops=0, bytes_accessed=6 << 20, transcendentals=0),
        name="pack_tokens",
    )(place, x, dy)


def repack_kernel(place, one, two, three, out, sems):
    other = columns((1 - place[1]) * HALF, HALF)
    copies = [(ref.at[:, :, other], out.at[i]) for i, ref in enumerate((one, two, three))]
    for copy in run_copies(copies, sems):
        copy.wait()


def repack(place, one, two, three):
    return pl.pallas_call(
        repack_kernel,
        out_shape=jax.ShapeDtypeStruct((3, 2, ROWS, HALF), BF16),
        in_specs=[SMEM] + [ANY] * 3,
        out_specs=ANY,
        scratch_shapes=[pltpu.SemaphoreType.DMA((3,))],
        cost_estimate=pl.CostEstimate(flops=0, bytes_accessed=2 << 20, transcendentals=0),
        name="repack_tokens",
    )(place, one, two, three)


def hidden_kernel(place, x, dy, beside, ups, downs, mine, theirs, xs, dys, sems):
    chip, core = place[0], place[1]
    copies = []
    for shift in range(CHIPS):
        own = columns(lax.rem(chip + shift, CHIPS) * WIDE + core * HALF, HALF)
        copies += [
            (x.at[:, own], xs.at[shift, :ROWS]),
            (dy.at[:, own], dys.at[shift, :ROWS]),
            (beside.at[shift, 0], xs.at[shift, ROWS:]),
            (beside.at[shift, 1], dys.at[shift, ROWS:]),
        ]
    for copy in run_copies(copies, sems):
        copy.wait()
    gate = up = dh = None
    for shift in range(CHIPS):
        a, b = xs[shift], dys[shift]
        g = jnp.dot(a, ups[:, shift, 0].reshape(HALF, HID), preferred_element_type=F32)
        u = jnp.dot(a, ups[:, shift, 1].reshape(HALF, HID), preferred_element_type=F32)
        d = sum(
            lax.dot_general(
                b[:, 256 * h : 256 * (h + 1)],
                downs[:, shift, h].reshape(HID, 256),
                (((1,), (1,)), ((), ())),
                preferred_element_type=F32,
            )
            for h in range(2)
        )
        gate, up, dh = (g, u, d) if gate is None else (gate + g, up + u, dh + d)
    for i, value in enumerate((gate, up, dh)):
        mine[i] = value[:ROWS]
        theirs[i] = value[ROWS:]


def hidden_sums(place, x, dy, beside, ups, downs):
    out = jax.ShapeDtypeStruct((3, ROWS, HID), F32)
    return pl.pallas_call(
        hidden_kernel,
        out_shape=(out, out),
        in_specs=[SMEM, ANY, ANY, ANY, VMEM, VMEM],
        out_specs=(VMEM, VMEM),
        scratch_shapes=[
            pltpu.VMEM((CHIPS, 2 * ROWS, HALF), BF16),
            pltpu.VMEM((CHIPS, 2 * ROWS, HALF), BF16),
            pltpu.SemaphoreType.DMA((16,)),
        ],
        compiler_params=pltpu.CompilerParams(vmem_limit_bytes=VMEM_LIMIT),
        cost_estimate=pl.CostEstimate(flops=6 * 256 * 2048 * 256, bytes_accessed=6 << 20, transcendentals=0),
        name="hidden_sums",
    )(place, x, dy, beside, ups, downs)


def activation_kernel(mine, arrived, out):
    gate = mine[0] + arrived[0]
    up = mine[1] + arrived[1]
    dh = mine[2] + arrived[2]
    sig = jax.nn.sigmoid(gate)
    active = gate * sig
    slope = sig * (1.0 + gate * (1.0 - sig))
    out[0] = (dh * up * slope).astype(BF16)
    out[1] = (dh * active).astype(BF16)
    out[2] = (active * up).astype(BF16)


def activation(mine, arrived):
    return pl.pallas_call(
        activation_kernel,
        out_shape=jax.ShapeDtypeStruct((3, ROWS, HID), BF16),
        in_specs=[VMEM, VMEM],
        out_specs=VMEM,
        cost_estimate=pl.CostEstimate(flops=20 * ROWS * HID, bytes_accessed=1 << 20, transcendentals=ROWS * HID),
        name="activation",
    )(mine, arrived)


def grads_kernel(place, x, dy, beside, one, two, three, swapped, *rest):
    acts, (gg, gu, gd, xs, dys, hs, sems) = rest[:8], rest[8:]
    chip, core = place[0], place[1]
    own = columns(chip * WIDE + core * HALF, HALF)
    half = columns(core * HALF, HALF)
    sources = [(x.at[:, own], dy.at[:, own])]
    sources += [(ref.at[0, :, half], ref.at[1, :, half]) for ref in (one, two, three)]
    sources += [(beside.at[0, 0], beside.at[0, 1])]
    sources += [(swapped.at[i, 0], swapped.at[i, 1]) for i in range(3)]
    copies = []
    for i, (a, b) in enumerate(sources):
        rows = pl.ds(i * ROWS, ROWS)
        copies += [(a, xs.at[rows]), (b, dys.at[rows]), (acts[i], hs.at[:, rows])]
    for copy in run_copies(copies, sems):
        copy.wait()
    tall = (((0,), (0,)), ((), ()))
    gg[0] = lax.dot_general(xs[...], hs[0], tall, preferred_element_type=F32).astype(BF16)
    gu[0] = lax.dot_general(xs[...], hs[1], tall, preferred_element_type=F32).astype(BF16)
    gd[0] = lax.dot_general(hs[2], dys[...], tall, preferred_element_type=F32).astype(BF16)


def grads(place, x, dy, beside, arrived, swapped, acts):
    tokens = 8 * ROWS
    return pl.pallas_call(
        grads_kernel,
        out_shape=(
            jax.ShapeDtypeStruct((1, HALF, HID), BF16),
            jax.ShapeDtypeStruct((1, HALF, HID), BF16),
            jax.ShapeDtypeStruct((1, HID, HALF), BF16),
        ),
        in_specs=[SMEM] + [ANY] * 15,
        out_specs=(VMEM,) * 3,
        scratch_shapes=[
            pltpu.VMEM((tokens, HALF), BF16),
            pltpu.VMEM((tokens, HALF), BF16),
            pltpu.VMEM((3, tokens, HID), BF16),
            pltpu.SemaphoreType.DMA((24,)),
        ],
        compiler_params=pltpu.CompilerParams(vmem_limit_bytes=VMEM_LIMIT),
        cost_estimate=pl.CostEstimate(flops=6 * 1024 * 512 * 256, bytes_accessed=5 << 20, transcendentals=0),
        name="weight_grads",
    )(place, x, dy, beside, *arrived, swapped, *acts)


def from_shift(value, shift):
    return lax.ppermute(value, "yh", [(i, (i - shift) % CHIPS) for i in range(CHIPS)])


def to_shift(value, shift):
    return lax.ppermute(value, "yh", [(i, (i + shift) % CHIPS) for i in range(CHIPS)])


def other_core(value):
    return lax.ppermute(value, "core", [(0, 1), (1, 0)])


def mean_of_replicas(delta):
    everyone = ("yl", "x", "z")
    count = lax.axis_size(everyone)
    rows, cols = delta.shape
    tiles = delta.reshape(rows // 8, 8, cols // 128, 128).transpose(0, 2, 1, 3).reshape(count, 8, 128)
    parts = lax.all_to_all(tiles, everyone, 0, 0, tiled=True)
    mean = jnp.sum(parts, axis=0, keepdims=True) / count
    whole = lax.all_to_all(jnp.broadcast_to(mean, (count, 8, 128)), everyone, 0, 0, tiled=True)
    return whole.reshape(rows // 8, cols // 128, 8, 128).transpose(0, 2, 1, 3).reshape(rows, cols)


def on_device(tokens, cotangent, w_gate, w_up, w_down, delta, anchor, momentum):
    x, dy = tokens[0], cotangent[0]
    place = jnp.stack([lax.axis_index("yh"), lax.axis_index("core")]).astype(jnp.int32)
    nx, nz = lax.axis_size("x"), lax.axis_size("z")
    gate_rows, down_rows = HALF // nx, HID // nz
    at_x, at_z = lax.axis_index("x") * gate_rows, lax.axis_index("z") * down_rows

    down = lax.dynamic_slice_in_dim(w_down, at_z, down_rows, 0)
    share = jnp.concatenate(
        [
            lax.dynamic_slice_in_dim(w_gate, at_x, gate_rows, 0),
            lax.dynamic_slice_in_dim(w_up, at_x, gate_rows, 0),
            down[:, :HID],
            down[:, HID:],
        ]
    )
    shares = [share] + [from_shift(share, s) for s in (1, 3, 2)]
    shares = [shares[i] for i in (0, 1, 3, 2)]
    cut = 2 * gate_rows
    ups = lax.all_gather(jnp.concatenate([s[:cut] for s in shares]), "x", axis=0, tiled=True)
    downs = lax.all_gather(jnp.concatenate([s[cut:] for s in shares]), "z", axis=0, tiled=True)
    ups = ups.reshape(nx, CHIPS, 2, gate_rows, HID)
    downs = downs.reshape(nz, CHIPS, 2, down_rows, HID)

    one, two, three, beside = pack(place, x, dy)
    one, three, two = to_shift(one, 1), to_shift(three, 3), to_shift(two, 2)
    beside = other_core(beside)
    swapped = other_core(repack(place, one, two, three))

    pseudo = mean_of_replicas(delta[0])
    new_momentum = 0.9 * momentum + pseudo
    new_anchor = anchor - 0.7 * (pseudo + 0.9 * new_momentum)

    mine, theirs = hidden_sums(place, x, dy, beside, ups, downs)
    acts = activation(mine, other_core(theirs))
    spread = [acts, to_shift(acts, 1), to_shift(acts, 2), to_shift(acts, 3)]
    spread += [other_core(a) for a in spread]
    grad_gate, grad_up, grad_down = grads(place, x, dy, beside, (one, two, three), swapped, spread)
    return grad_gate, grad_up, grad_down, new_anchor, new_momentum


def solution(mesh):
    fine = Mesh(mesh.devices.reshape(4, 2, 2, 4, 8), ("yh", "core", "yl", "x", "z"))
    fsdp, replica = ("yh", "core"), ("yl", "x", "z")
    placed = (
        P(replica, fsdp, None),
        P(replica, fsdp, None),
        P(fsdp, None),
        P(fsdp, None),
        P(None, fsdp),
        P(replica, fsdp, None),
        P(fsdp, None),
        P(fsdp, None),
    )
    return jax.shard_map(
        on_device,
        mesh=fine,
        in_specs=placed,
        out_specs=(
            P(replica, fsdp, None),
            P(replica, fsdp, None),
            P(replica, None, fsdp),
            P(fsdp, None),
            P(fsdp, None),
        ),
        check_vma=False,
    )
```

```python
import functools

import jax
import jax.numpy as jnp
from jax import lax
from jax.experimental import pallas as pl
from jax.experimental.pallas import tpu as pltpu
from jax.sharding import Mesh
from jax.sharding import PartitionSpec as P

CHIPS = 4
ROWS = 128
WIDE = 1024
HALF = 512
HID = 256
VMEM_LIMIT = 48 * 1024 * 1024

F32 = jnp.float32
BF16 = jnp.bfloat16
ANY = pl.BlockSpec(memory_space=pl.ANY)
VMEM = pl.BlockSpec(memory_space=pltpu.VMEM)
SMEM = pl.BlockSpec(memory_space=pltpu.SMEM)


def run_copies(copies, sems):
    started = [pltpu.make_async_copy(src, dst, sems.at[i]) for i, (src, dst) in enumerate(copies)]
    for copy in started:
        copy.start()
    for copy in started:
        copy.wait()


def columns(base):
    return pl.ds(pl.multiple_of(base, HALF), HALF)


def wide_columns(chip):
    return pl.ds(pl.multiple_of(chip * WIDE, WIDE), WIDE)


def share_kernel(parts, place, gate, up, down, out, sems):
    gate_rows, down_rows = HALF // parts, HID // parts
    at_gate = pl.ds(pl.multiple_of(place[1] * gate_rows, gate_rows), gate_rows)
    at_down = pl.ds(pl.multiple_of(place[1] * down_rows, down_rows), down_rows)
    copies = []
    for chip in range(CHIPS):
        to = out.at[chip]
        copies += [
            (gate.at[at_gate], to.at[pl.ds(0, gate_rows)]),
            (up.at[at_gate], to.at[pl.ds(gate_rows, gate_rows)]),
            (down.at[at_down, :HID], to.at[pl.ds(2 * gate_rows, down_rows)]),
            (down.at[at_down, HID:], to.at[pl.ds(2 * gate_rows + down_rows, down_rows)]),
        ]
    run_copies(copies, sems)


def own_share(place, gate, up, down, parts):
    rows = 2 * (HALF + HID) // parts
    return pl.pallas_call(
        functools.partial(share_kernel, parts),
        out_shape=jax.ShapeDtypeStruct((CHIPS, rows, HID), BF16),
        in_specs=[SMEM, ANY, ANY, ANY],
        out_specs=VMEM,
        scratch_shapes=[pltpu.SemaphoreType.DMA((16,))],
        cost_estimate=pl.CostEstimate(flops=0, bytes_accessed=2 << 20, transcendentals=0),
        name="weight_share",
    )(place, gate, up, down)


def pack_kernel(shifts, place, x, dy, after, *rest):
    outs, sems = rest[:-1], rest[-1]
    del after
    copies = []
    for shift, out in zip(shifts, outs):
        block = wide_columns(lax.rem(place[2] + shift, CHIPS))
        copies += [(x.at[:, block], out.at[0]), (dy.at[:, block], out.at[1])]
    if len(outs) > len(shifts):
        for chip in range(CHIPS):
            other = columns(chip * WIDE + (1 - place[0]) * HALF)
            copies += [(x.at[:, other], outs[-1].at[chip, 0]), (dy.at[:, other], outs[-1].at[chip, 1])]
    run_copies(copies, sems)


def pack(place, x, dy, after, shifts, with_beside):
    outs = [jax.ShapeDtypeStruct((2, ROWS, WIDE), BF16)] * len(shifts)
    if with_beside:
        outs.append(jax.ShapeDtypeStruct((CHIPS, 2, ROWS, HALF), BF16))
    return pl.pallas_call(
        functools.partial(pack_kernel, shifts),
        out_shape=tuple(outs),
        in_specs=[SMEM, ANY, ANY, ANY],
        out_specs=(VMEM,) * len(outs),
        scratch_shapes=[pltpu.SemaphoreType.DMA((2 * len(shifts) + 8 * with_beside,))],
        compiler_params=pltpu.CompilerParams(vmem_limit_bytes=VMEM_LIMIT),
        cost_estimate=pl.CostEstimate(flops=0, bytes_accessed=len(outs) << 20, transcendentals=0),
        name="pack_tokens",
    )(place, x, dy, after)


def repack_kernel(place, one, two, three, out, sems):
    other = columns((1 - place[0]) * HALF)
    run_copies([(ref.at[:, :, other], out.at[i]) for i, ref in enumerate((one, two, three))], sems)


def repack(place, arrived):
    return pl.pallas_call(
        repack_kernel,
        out_shape=jax.ShapeDtypeStruct((CHIPS - 1, 2, ROWS, HALF), BF16),
        in_specs=[SMEM] + [ANY] * 3,
        out_specs=VMEM,
        scratch_shapes=[pltpu.SemaphoreType.DMA((CHIPS - 1,))],
        compiler_params=pltpu.CompilerParams(vmem_limit_bytes=VMEM_LIMIT),
        cost_estimate=pl.CostEstimate(flops=0, bytes_accessed=2 << 20, transcendentals=0),
        name="repack_tokens",
    )(place, *arrived)


def tiles_kernel(delta, after, out, sems):
    del after
    rows, cols = delta.shape
    copies = []
    for i in range(rows // 8):
        for j in range(cols // 128):
            copies.append((delta.at[8 * i : 8 * i + 8, 128 * j : 128 * j + 128], out.at[i * (cols // 128) + j]))
    run_copies(copies, sems)


def tiles_of(delta, after):
    count = delta.size // 1024
    return pl.pallas_call(
        tiles_kernel,
        out_shape=jax.ShapeDtypeStruct((count, 8, 128), F32),
        in_specs=[ANY, ANY],
        out_specs=VMEM,
        scratch_shapes=[pltpu.SemaphoreType.DMA((count,))],
        cost_estimate=pl.CostEstimate(flops=0, bytes_accessed=1 << 19, transcendentals=0),
        name="delta_tiles",
    )(delta, after)


def hidden_kernel(waited, place, x, dy, beside, *rest):
    rest = rest[waited:]
    weights, (mine, theirs, xs, dys, gates, ups, downs, sems) = rest[:-8], rest[-8:]
    parts = len(weights)
    gate_rows, down_rows = HALF // parts, HID // parts
    core, at = place[0], place[1]
    copies = []
    for shift, ref in enumerate(weights):
        part = lax.rem(at + shift, parts)
        to_gate = pl.ds(pl.multiple_of(part * gate_rows, gate_rows), gate_rows)
        to_down = pl.ds(pl.multiple_of(part * down_rows, down_rows), down_rows)
        copies += [
            (ref.at[:, pl.ds(0, gate_rows)], gates.at[:, to_gate]),
            (ref.at[:, pl.ds(gate_rows, gate_rows)], ups.at[:, to_gate]),
            (ref.at[:, pl.ds(2 * gate_rows, down_rows)], downs.at[:, 0, to_down]),
            (ref.at[:, pl.ds(2 * gate_rows + down_rows, down_rows)], downs.at[:, 1, to_down]),
        ]
    for chip in range(CHIPS):
        own = columns(chip * WIDE + core * HALF)
        copies += [
            (x.at[:, own], xs.at[chip, :ROWS]),
            (dy.at[:, own], dys.at[chip, :ROWS]),
            (beside.at[chip, 0], xs.at[chip, ROWS:]),
            (beside.at[chip, 1], dys.at[chip, ROWS:]),
        ]
    run_copies(copies, sems)
    gate = up = dh = 0.0
    for chip in range(CHIPS):
        a, b = xs[chip], dys[chip]
        gate += jnp.dot(a, gates[chip], preferred_element_type=F32)
        up += jnp.dot(a, ups[chip], preferred_element_type=F32)
        for h in range(2):
            dh += lax.dot_general(
                b[:, HID * h : HID * (h + 1)],
                downs[chip, h],
                (((1,), (1,)), ((), ())),
                preferred_element_type=F32,
            )
    for i, value in enumerate((gate, up, dh)):
        mine[i] = value[:ROWS]
        theirs[i] = value[ROWS:]


def hidden_sums(place, x, dy, beside, weights, after):
    out = jax.ShapeDtypeStruct((3, ROWS, HID), F32)
    return pl.pallas_call(
        functools.partial(hidden_kernel, len(after)),
        out_shape=(out, out),
        in_specs=[SMEM] + [ANY] * (3 + len(after) + len(weights)),
        out_specs=(VMEM, VMEM),
        scratch_shapes=[
            pltpu.VMEM((CHIPS, 2 * ROWS, HALF), BF16),
            pltpu.VMEM((CHIPS, 2 * ROWS, HALF), BF16),
            pltpu.VMEM((CHIPS, HALF, HID), BF16),
            pltpu.VMEM((CHIPS, HALF, HID), BF16),
            pltpu.VMEM((CHIPS, 2, HID, HID), BF16),
            pltpu.SemaphoreType.DMA((4 * len(weights) + 16,)),
        ],
        compiler_params=pltpu.CompilerParams(vmem_limit_bytes=VMEM_LIMIT),
        cost_estimate=pl.CostEstimate(flops=6 * 256 * 2048 * 256, bytes_accessed=6 << 20, transcendentals=0),
        name="hidden_sums",
    )(place, x, dy, beside, *after, *weights)


def activation_kernel(mine, arrived, out):
    gate = mine[0] + arrived[0]
    up = mine[1] + arrived[1]
    dh = mine[2] + arrived[2]
    sig = jax.nn.sigmoid(gate)
    active = gate * sig
    slope = sig * (1.0 + gate * (1.0 - sig))
    for i, value in enumerate((dh * up * slope, dh * active, active * up)):
        for chip in range(CHIPS):
            out[chip, i] = value.astype(BF16)


def activation(mine, arrived):
    return pl.pallas_call(
        activation_kernel,
        out_shape=jax.ShapeDtypeStruct((CHIPS, 3, ROWS, HID), BF16),
        in_specs=[VMEM, VMEM],
        out_specs=VMEM,
        cost_estimate=pl.CostEstimate(flops=20 * ROWS * HID, bytes_accessed=1 << 20, transcendentals=ROWS * HID),
        name="activation",
    )(mine, arrived)


def grads_kernel(place, x, dy, beside, one, two, three, swapped, acts, acts_beside, gg, gu, gd, xs, dys, hs, sems):
    core, chip = place[0], place[2]
    half, own = columns(core * HALF), columns(chip * WIDE + core * HALF)
    copies = []
    for i, ref in enumerate((None, one, two, three)):
        source = lax.rem(chip + CHIPS - i, CHIPS)
        near = pl.ds(pl.multiple_of(source * ROWS, ROWS), ROWS)
        far = pl.ds(pl.multiple_of((CHIPS + source) * ROWS, ROWS), ROWS)
        if i:
            copies += [(ref.at[0, :, half], xs.at[near]), (ref.at[1, :, half], dys.at[near])]
            copies += [(swapped.at[i - 1, 0], xs.at[far]), (swapped.at[i - 1, 1], dys.at[far])]
        else:
            copies += [(x.at[:, own], xs.at[near]), (dy.at[:, own], dys.at[near])]
            copies += [(beside.at[chip, 0], xs.at[far]), (beside.at[chip, 1], dys.at[far])]
        near, far = pl.ds(i * ROWS, ROWS), pl.ds((CHIPS + i) * ROWS, ROWS)
        copies += [(acts.at[i], hs.at[:, near]), (acts_beside.at[i], hs.at[:, far])]
    run_copies(copies, sems)
    tall = (((0,), (0,)), ((), ()))
    gg[0] = lax.dot_general(xs[...], hs[0], tall, preferred_element_type=F32).astype(BF16)
    gu[0] = lax.dot_general(xs[...], hs[1], tall, preferred_element_type=F32).astype(BF16)
    gd[0] = lax.dot_general(hs[2], dys[...], tall, preferred_element_type=F32).astype(BF16)


def grads(place, x, dy, beside, arrived, swapped, acts, acts_beside):
    tokens = 2 * CHIPS * ROWS
    return pl.pallas_call(
        grads_kernel,
        out_shape=(
            jax.ShapeDtypeStruct((1, HALF, HID), BF16),
            jax.ShapeDtypeStruct((1, HALF, HID), BF16),
            jax.ShapeDtypeStruct((1, HID, HALF), BF16),
        ),
        in_specs=[SMEM] + [ANY] * 9,
        out_specs=(VMEM,) * 3,
        scratch_shapes=[
            pltpu.VMEM((tokens, HALF), BF16),
            pltpu.VMEM((tokens, HALF), BF16),
            pltpu.VMEM((3, tokens, HID), BF16),
            pltpu.SemaphoreType.DMA((24,)),
        ],
        compiler_params=pltpu.CompilerParams(vmem_limit_bytes=VMEM_LIMIT),
        cost_estimate=pl.CostEstimate(flops=6 * 1024 * 512 * 256, bytes_accessed=5 << 20, transcendentals=0),
        name="weight_grads",
    )(place, x, dy, beside, *arrived, swapped, acts, acts_beside)


def to_chips(value):
    return lax.all_to_all(value, "yh", 0, 0, tiled=True)


def to_shift(value, shift):
    return lax.ppermute(value, "yh", [(i, (i + shift) % CHIPS) for i in range(CHIPS)])


def other_core(value):
    return lax.ppermute(value, "core", [(0, 1), (1, 0)])


def from_x(value, shift, size):
    return lax.ppermute(value, "x", [(i, (i - shift) % size) for i in range(size)])


def mean_of_replicas(delta, after):
    everyone = ("yl", "x", "z")
    count = lax.axis_size(everyone)
    rows, cols = delta.shape
    parts = lax.all_to_all(tiles_of(delta, after), everyone, 0, 0, tiled=True)
    mean = jnp.sum(parts, axis=0, keepdims=True) / count
    whole = lax.all_to_all(jnp.broadcast_to(mean, (count, 8, 128)), everyone, 0, 0, tiled=True)
    return whole.reshape(rows // 8, cols // 128, 8, 128).transpose(0, 2, 1, 3).reshape(rows, cols)


def on_device(tokens, cotangent, w_gate, w_up, w_down, delta, anchor, momentum):
    x, dy = tokens[0], cotangent[0]
    place = jnp.stack([lax.axis_index(name) for name in ("core", "x", "yh")]).astype(jnp.int32)
    parts = lax.axis_size("x")

    outgoing = own_share(place, w_gate, w_up, w_down, parts)
    share = to_chips(outgoing)
    weights = [share] + [from_x(share, shift, parts) for shift in range(1, parts)]

    (two,) = pack(place, x, dy, outgoing, (2,), False)
    one, three, beside = pack(place, x, dy, share, (1, 3), True)
    arrived = [to_shift(one, 1), to_shift(two, 2), to_shift(three, 3)]
    beside = other_core(beside)
    swapped = other_core(repack(place, arrived))

    pseudo = mean_of_replicas(delta[0], beside)
    new_momentum = 0.9 * momentum + pseudo
    new_anchor = anchor - 0.7 * (pseudo + 0.9 * new_momentum)

    mine, theirs = hidden_sums(place, x, dy, beside, weights, (*arrived, pseudo))
    acts = to_chips(activation(mine, other_core(theirs)))
    grad_gate, grad_up, grad_down = grads(place, x, dy, beside, arrived, swapped, acts, other_core(acts))
    return grad_gate, grad_up, grad_down, new_anchor, new_momentum


def solution(mesh):
    fine = Mesh(mesh.devices.reshape(4, 2, 2, 4, 8), ("yh", "core", "yl", "x", "z"))
    fsdp, replica = ("yh", "core"), ("yl", "x", "z")
    placed = (
        P(replica, fsdp, None),
        P(replica, fsdp, None),
        P(fsdp, None),
        P(fsdp, None),
        P(None, fsdp),
        P(replica, fsdp, None),
        P(fsdp, None),
        P(fsdp, None),
    )
    return jax.shard_map(
        on_device,
        mesh=fine,
        in_specs=placed,
        out_specs=(
            P(replica, fsdp, None),
            P(replica, fsdp, None),
            P(replica, None, fsdp),
            P(fsdp, None),
            P(fsdp, None),
        ),
        check_vma=False,
    )
```

```python
import functools

import jax
import jax.numpy as jnp
from jax import lax
from jax.experimental import pallas as pl
from jax.experimental.pallas import tpu as pltpu
from jax.sharding import Mesh
from jax.sharding import PartitionSpec as P

CHIPS = 4
ROWS = 128
WIDE = 1024
HALF = 512
HID = 256
VMEM_LIMIT = 48 * 1024 * 1024

F32 = jnp.float32
BF16 = jnp.bfloat16
ANY = pl.BlockSpec(memory_space=pl.ANY)
VMEM = pl.BlockSpec(memory_space=pltpu.VMEM)
SMEM = pl.BlockSpec(memory_space=pltpu.SMEM)


def run_copies(copies, sems):
    started = [pltpu.make_async_copy(src, dst, sems.at[i]) for i, (src, dst) in enumerate(copies)]
    for copy in started:
        copy.start()
    for copy in started:
        copy.wait()


def columns(base):
    return pl.ds(pl.multiple_of(base, HALF), HALF)


def wide_columns(chip):
    return pl.ds(pl.multiple_of(chip * WIDE, WIDE), WIDE)


def share_kernel(parts, place, gate, up, down, out, sems):
    gate_rows, down_rows = HALF // parts, HID // parts
    cut = 2 * gate_rows
    at_gate = pl.ds(pl.multiple_of(place[1] * gate_rows, gate_rows), gate_rows)
    at_down = pl.ds(pl.multiple_of(place[1] * down_rows, down_rows), down_rows)
    copies = [
        (gate.at[at_gate], out.at[pl.ds(0, gate_rows)]),
        (up.at[at_gate], out.at[pl.ds(gate_rows, gate_rows)]),
        (down.at[at_down, :HID], out.at[pl.ds(cut, down_rows)]),
        (down.at[at_down, HID:], out.at[pl.ds(cut + down_rows, down_rows)]),
    ]
    run_copies(copies, sems)


def own_share(place, gate, up, down, parts):
    return pl.pallas_call(
        functools.partial(share_kernel, parts),
        out_shape=jax.ShapeDtypeStruct((2 * (HALF + HID) // parts, HID), BF16),
        in_specs=[SMEM, ANY, ANY, ANY],
        out_specs=VMEM,
        scratch_shapes=[pltpu.SemaphoreType.DMA((4,))],
        cost_estimate=pl.CostEstimate(flops=0, bytes_accessed=1 << 18, transcendentals=0),
        name="weight_share",
    )(place, gate, up, down)


def pack_kernel(shifts, place, x, dy, after, *rest):
    outs, sems = rest[:-1], rest[-1]
    del after
    copies = []
    for shift, out in zip(shifts, outs):
        block = wide_columns(lax.rem(place[2] + shift, CHIPS))
        copies += [(x.at[:, block], out.at[0]), (dy.at[:, block], out.at[1])]
    if len(outs) > len(shifts):
        for chip in range(CHIPS):
            other = columns(chip * WIDE + (1 - place[0]) * HALF)
            copies += [(x.at[:, other], outs[-1].at[chip, 0]), (dy.at[:, other], outs[-1].at[chip, 1])]
    run_copies(copies, sems)


def pack(place, x, dy, after, shifts, with_beside):
    outs = [jax.ShapeDtypeStruct((2, ROWS, WIDE), BF16)] * len(shifts)
    if with_beside:
        outs.append(jax.ShapeDtypeStruct((CHIPS, 2, ROWS, HALF), BF16))
    return pl.pallas_call(
        functools.partial(pack_kernel, shifts),
        out_shape=tuple(outs),
        in_specs=[SMEM, ANY, ANY, ANY],
        out_specs=(VMEM,) * len(outs),
        scratch_shapes=[pltpu.SemaphoreType.DMA((2 * len(shifts) + 8 * with_beside,))],
        compiler_params=pltpu.CompilerParams(vmem_limit_bytes=VMEM_LIMIT),
        cost_estimate=pl.CostEstimate(flops=0, bytes_accessed=len(outs) << 20, transcendentals=0),
        name="pack_tokens",
    )(place, x, dy, after)


def repack_kernel(place, one, two, three, out, sems):
    other = columns((1 - place[0]) * HALF)
    run_copies([(ref.at[:, :, other], out.at[i]) for i, ref in enumerate((one, two, three))], sems)


def repack(place, arrived):
    return pl.pallas_call(
        repack_kernel,
        out_shape=jax.ShapeDtypeStruct((CHIPS - 1, 2, ROWS, HALF), BF16),
        in_specs=[SMEM] + [ANY] * 3,
        out_specs=VMEM,
        scratch_shapes=[pltpu.SemaphoreType.DMA((CHIPS - 1,))],
        compiler_params=pltpu.CompilerParams(vmem_limit_bytes=VMEM_LIMIT),
        cost_estimate=pl.CostEstimate(flops=0, bytes_accessed=2 << 20, transcendentals=0),
        name="repack_tokens",
    )(place, *arrived)


def tiles_kernel(delta, after, out, sems):
    del after
    rows, cols = delta.shape
    copies = []
    for i in range(rows // 8):
        for j in range(cols // 128):
            copies.append((delta.at[8 * i : 8 * i + 8, 128 * j : 128 * j + 128], out.at[i * (cols // 128) + j]))
    run_copies(copies, sems)


def tiles_of(delta, after):
    count = delta.size // 1024
    return pl.pallas_call(
        tiles_kernel,
        out_shape=jax.ShapeDtypeStruct((count, 8, 128), F32),
        in_specs=[ANY, ANY],
        out_specs=VMEM,
        scratch_shapes=[pltpu.SemaphoreType.DMA((count,))],
        cost_estimate=pl.CostEstimate(flops=0, bytes_accessed=1 << 19, transcendentals=0),
        name="delta_tiles",
    )(delta, after)


def hidden_kernel(waited, place, x, dy, beside, weights, *rest):
    mine, theirs, xs, dys, gates, ups, downs, sems = rest[waited:]
    parts = weights.shape[0]
    gate_rows, down_rows = HALF // parts, HID // parts
    cut = 2 * gate_rows
    copies = []
    for shift in range(CHIPS):
        chip = lax.rem(place[2] + shift, CHIPS)
        own = columns(chip * WIDE + place[0] * HALF)
        copies += [
            (x.at[:, own], xs.at[shift, :ROWS]),
            (dy.at[:, own], dys.at[shift, :ROWS]),
            (beside.at[chip, 0], xs.at[shift, ROWS:]),
            (beside.at[chip, 1], dys.at[shift, ROWS:]),
        ]
    for part in range(parts):
        ref = weights.at[part]
        to_gate, to_down = pl.ds(part * gate_rows, gate_rows), pl.ds(part * down_rows, down_rows)
        copies += [
            (ref.at[:, pl.ds(0, gate_rows)], gates.at[:, to_gate]),
            (ref.at[:, pl.ds(gate_rows, gate_rows)], ups.at[:, to_gate]),
            (ref.at[:, pl.ds(cut, down_rows)], downs.at[:, 0, to_down]),
            (ref.at[:, pl.ds(cut + down_rows, down_rows)], downs.at[:, 1, to_down]),
        ]
    run_copies(copies, sems)
    gate = up = dh = 0.0
    for chip in range(CHIPS):
        a, b = xs[chip], dys[chip]
        gate += jnp.dot(a, gates[chip], preferred_element_type=F32)
        up += jnp.dot(a, ups[chip], preferred_element_type=F32)
        for h in range(2):
            dh += lax.dot_general(
                b[:, HID * h : HID * (h + 1)],
                downs[chip, h],
                (((1,), (1,)), ((), ())),
                preferred_element_type=F32,
            )
    for i, value in enumerate((gate, up, dh)):
        mine[i] = value[:ROWS]
        theirs[i] = value[ROWS:]


def hidden_sums(place, x, dy, beside, weights, after):
    out = jax.ShapeDtypeStruct((3, ROWS, HID), F32)
    return pl.pallas_call(
        functools.partial(hidden_kernel, len(after)),
        out_shape=(out, out),
        in_specs=[SMEM] + [ANY] * (4 + len(after)),
        out_specs=(VMEM, VMEM),
        scratch_shapes=[
            pltpu.VMEM((CHIPS, 2 * ROWS, HALF), BF16),
            pltpu.VMEM((CHIPS, 2 * ROWS, HALF), BF16),
            pltpu.VMEM((CHIPS, HALF, HID), BF16),
            pltpu.VMEM((CHIPS, HALF, HID), BF16),
            pltpu.VMEM((CHIPS, 2, HID, HID), BF16),
            pltpu.SemaphoreType.DMA((4 * weights.shape[0] + 16,)),
        ],
        compiler_params=pltpu.CompilerParams(vmem_limit_bytes=VMEM_LIMIT),
        cost_estimate=pl.CostEstimate(flops=6 * 256 * 2048 * 256, bytes_accessed=6 << 20, transcendentals=0),
        name="hidden_sums",
    )(place, x, dy, beside, weights, *after)


def activation_kernel(mine_ref, arrived_ref, after, out, mine, arrived, sems):
    del after
    run_copies([(mine_ref, mine), (arrived_ref, arrived)], sems)
    gate = mine[0] + arrived[0]
    up = mine[1] + arrived[1]
    dh = mine[2] + arrived[2]
    sig = jax.nn.sigmoid(gate)
    active = gate * sig
    slope = sig * (1.0 + gate * (1.0 - sig))
    for i, value in enumerate((dh * up * slope, dh * active, active * up)):
        for chip in range(CHIPS):
            out[chip, i] = value.astype(BF16)


def activation(mine, arrived, after):
    return pl.pallas_call(
        activation_kernel,
        out_shape=jax.ShapeDtypeStruct((CHIPS, 3, ROWS, HID), BF16),
        in_specs=[ANY] * 3,
        out_specs=VMEM,
        scratch_shapes=[
            pltpu.VMEM((3, ROWS, HID), F32),
            pltpu.VMEM((3, ROWS, HID), F32),
            pltpu.SemaphoreType.DMA((2,)),
        ],
        cost_estimate=pl.CostEstimate(flops=20 * ROWS * HID, bytes_accessed=1 << 20, transcendentals=ROWS * HID),
        name="activation",
    )(mine, arrived, after)


def grads_kernel(place, x, dy, beside, one, two, three, swapped, acts, acts_beside, gg, gu, gd, xs, dys, hs, sems):
    core, chip = place[0], place[2]
    half, own = columns(core * HALF), columns(chip * WIDE + core * HALF)
    copies = []
    for i, ref in enumerate((None, one, two, three)):
        source = lax.rem(chip + CHIPS - i, CHIPS)
        near = pl.ds(pl.multiple_of(source * ROWS, ROWS), ROWS)
        far = pl.ds(pl.multiple_of((CHIPS + source) * ROWS, ROWS), ROWS)
        if i:
            copies += [(ref.at[0, :, half], xs.at[near]), (ref.at[1, :, half], dys.at[near])]
            copies += [(swapped.at[i - 1, 0], xs.at[far]), (swapped.at[i - 1, 1], dys.at[far])]
        else:
            copies += [(x.at[:, own], xs.at[near]), (dy.at[:, own], dys.at[near])]
            copies += [(beside.at[chip, 0], xs.at[far]), (beside.at[chip, 1], dys.at[far])]
        near, far = pl.ds(i * ROWS, ROWS), pl.ds((CHIPS + i) * ROWS, ROWS)
        copies += [(acts.at[i], hs.at[:, near]), (acts_beside.at[i], hs.at[:, far])]
    run_copies(copies, sems)
    tall = (((0,), (0,)), ((), ()))
    gg[0] = lax.dot_general(xs[...], hs[0], tall, preferred_element_type=F32).astype(BF16)
    gu[0] = lax.dot_general(xs[...], hs[1], tall, preferred_element_type=F32).astype(BF16)
    gd[0] = lax.dot_general(hs[2], dys[...], tall, preferred_element_type=F32).astype(BF16)


def grads(place, x, dy, beside, arrived, swapped, acts, acts_beside):
    tokens = 2 * CHIPS * ROWS
    return pl.pallas_call(
        grads_kernel,
        out_shape=(
            jax.ShapeDtypeStruct((1, HALF, HID), BF16),
            jax.ShapeDtypeStruct((1, HALF, HID), BF16),
            jax.ShapeDtypeStruct((1, HID, HALF), BF16),
        ),
        in_specs=[SMEM] + [ANY] * 9,
        out_specs=(VMEM,) * 3,
        scratch_shapes=[
            pltpu.VMEM((tokens, HALF), BF16),
            pltpu.VMEM((tokens, HALF), BF16),
            pltpu.VMEM((3, tokens, HID), BF16),
            pltpu.SemaphoreType.DMA((24,)),
        ],
        compiler_params=pltpu.CompilerParams(vmem_limit_bytes=VMEM_LIMIT),
        cost_estimate=pl.CostEstimate(flops=6 * 1024 * 512 * 256, bytes_accessed=5 << 20, transcendentals=0),
        name="weight_grads",
    )(place, x, dy, beside, *arrived, swapped, acts, acts_beside)


def to_chips(value):
    return lax.all_to_all(value, "yh", 0, 0, tiled=True)


def to_shift(value, shift):
    return lax.ppermute(value, "yh", [(i, (i + shift) % CHIPS) for i in range(CHIPS)])


def from_shift(value, shift):
    return lax.ppermute(value, "yh", [(i, (i - shift) % CHIPS) for i in range(CHIPS)])


def other_core(value):
    return lax.ppermute(value, "core", [(0, 1), (1, 0)])


def mean_of_replicas(delta, after):
    everyone = ("yl", "x", "z")
    count = lax.axis_size(everyone)
    rows, cols = delta.shape
    parts = lax.all_to_all(tiles_of(delta, after), everyone, 0, 0, tiled=True)
    mean = jnp.sum(parts, axis=0, keepdims=True) / count
    whole = lax.all_to_all(jnp.broadcast_to(mean, (count, 8, 128)), everyone, 0, 0, tiled=True)
    return whole.reshape(rows // 8, cols // 128, 8, 128).transpose(0, 2, 1, 3).reshape(rows, cols)


def on_device(tokens, cotangent, w_gate, w_up, w_down, delta, anchor, momentum):
    x, dy = tokens[0], cotangent[0]
    place = jnp.stack([lax.axis_index(name) for name in ("core", "z", "yh")]).astype(jnp.int32)
    parts = lax.axis_size("z")

    share = own_share(place, w_gate, w_up, w_down, parts)
    shares = {shift: from_shift(share, shift) for shift in (2, 1, 3)}
    first = shares[2]
    shares = jnp.stack([share] + [shares[shift] for shift in (1, 2, 3)])
    weights = lax.all_gather(shares, "z", axis=0, tiled=False)

    one, two, three, beside = pack(place, x, dy, shares, (1, 2, 3), True)
    arrived = [to_shift(one, 1), to_shift(two, 2), to_shift(three, 3)]
    beside = other_core(beside)
    swapped = other_core(repack(place, arrived))

    pseudo = mean_of_replicas(delta[0], first)
    new_momentum = 0.9 * momentum + pseudo
    new_anchor = anchor - 0.7 * (pseudo + 0.9 * new_momentum)

    mine, theirs = hidden_sums(place, x, dy, beside, weights, arrived)
    acts = to_chips(activation(mine, other_core(theirs), new_anchor))
    grad_gate, grad_up, grad_down = grads(place, x, dy, beside, arrived, swapped, acts, other_core(acts))
    return grad_gate, grad_up, grad_down, new_anchor, new_momentum


def solution(mesh):
    fine = Mesh(mesh.devices.reshape(4, 2, 2, 4, 8), ("yh", "core", "yl", "x", "z"))
    fsdp, replica = ("yh", "core"), ("yl", "x", "z")
    placed = (
        P(replica, fsdp, None),
        P(replica, fsdp, None),
        P(fsdp, None),
        P(fsdp, None),
        P(None, fsdp),
        P(replica, fsdp, None),
        P(fsdp, None),
        P(fsdp, None),
    )
    return jax.shard_map(
        on_device,
        mesh=fine,
        in_specs=placed,
        out_specs=(
            P(replica, fsdp, None),
            P(replica, fsdp, None),
            P(replica, None, fsdp),
            P(fsdp, None),
            P(fsdp, None),
        ),
        check_vma=False,
    )
```

```python
import functools

import jax
import jax.numpy as jnp
from jax import lax
from jax.experimental import pallas as pl
from jax.experimental.pallas import tpu as pltpu
from jax.sharding import Mesh
from jax.sharding import PartitionSpec as P

CHIPS = 4
ROWS = 128
WIDE = 1024
HALF = 512
HID = 256
VMEM_LIMIT = 48 * 1024 * 1024

F32 = jnp.float32
BF16 = jnp.bfloat16
ANY = pl.BlockSpec(memory_space=pl.ANY)
VMEM = pl.BlockSpec(memory_space=pltpu.VMEM)
SMEM = pl.BlockSpec(memory_space=pltpu.SMEM)


def run_copies(copies, sems):
    started = [pltpu.make_async_copy(src, dst, sems.at[i]) for i, (src, dst) in enumerate(copies)]
    for copy in started:
        copy.start()
    for copy in started:
        copy.wait()


def columns(base):
    return pl.ds(pl.multiple_of(base, HALF), HALF)


def share_kernel(parts, place, gate, up, down, out, sems):
    gate_rows, down_rows = HALF // parts, HID // parts
    cut = 2 * gate_rows
    at_gate = pl.ds(pl.multiple_of(place[1] * gate_rows, gate_rows), gate_rows)
    at_down = pl.ds(pl.multiple_of(place[1] * down_rows, down_rows), down_rows)
    copies = [
        (gate.at[at_gate], out.at[pl.ds(0, gate_rows)]),
        (up.at[at_gate], out.at[pl.ds(gate_rows, gate_rows)]),
        (down.at[at_down, :HID], out.at[pl.ds(cut, down_rows)]),
        (down.at[at_down, HID:], out.at[pl.ds(cut + down_rows, down_rows)]),
    ]
    run_copies(copies, sems)


def own_share(place, gate, up, down, parts):
    return pl.pallas_call(
        functools.partial(share_kernel, parts),
        out_shape=jax.ShapeDtypeStruct((2 * (HALF + HID) // parts, HID), BF16),
        in_specs=[SMEM, ANY, ANY, ANY],
        out_specs=VMEM,
        scratch_shapes=[pltpu.SemaphoreType.DMA((4,))],
        cost_estimate=pl.CostEstimate(flops=0, bytes_accessed=1 << 18, transcendentals=0),
        name="weight_share",
    )(place, gate, up, down)


def pack_kernel(place, x, dy, after, also_after, out, beside, sems):
    del after, also_after
    other = (1 - place[0]) * HALF
    copies = []
    for chip in range(CHIPS):
        for i, ref in enumerate((x, dy)):
            copies += [
                (ref.at[:, pl.ds(chip * WIDE, WIDE)], out.at[chip, i]),
                (ref.at[:, columns(chip * WIDE + other)], beside.at[chip, i]),
            ]
    run_copies(copies, sems)


def pack(place, x, dy, after, also_after):
    return pl.pallas_call(
        pack_kernel,
        out_shape=(
            jax.ShapeDtypeStruct((CHIPS, 2, ROWS, WIDE), BF16),
            jax.ShapeDtypeStruct((CHIPS, 2, ROWS, HALF), BF16),
        ),
        in_specs=[SMEM] + [ANY] * 4,
        out_specs=(VMEM,) * 2,
        scratch_shapes=[pltpu.SemaphoreType.DMA((16,))],
        compiler_params=pltpu.CompilerParams(vmem_limit_bytes=VMEM_LIMIT),
        cost_estimate=pl.CostEstimate(flops=0, bytes_accessed=6 << 20, transcendentals=0),
        name="pack_tokens",
    )(place, x, dy, after, also_after)


def repack_kernel(place, arrived, out, sems):
    other = columns((1 - place[0]) * HALF)
    run_copies([(arrived.at[i, :, :, other], out.at[i]) for i in range(CHIPS)], sems)


def repack(place, arrived):
    return pl.pallas_call(
        repack_kernel,
        out_shape=jax.ShapeDtypeStruct((CHIPS, 2, ROWS, HALF), BF16),
        in_specs=[SMEM, ANY],
        out_specs=VMEM,
        scratch_shapes=[pltpu.SemaphoreType.DMA((CHIPS,))],
        compiler_params=pltpu.CompilerParams(vmem_limit_bytes=VMEM_LIMIT),
        cost_estimate=pl.CostEstimate(flops=0, bytes_accessed=2 << 20, transcendentals=0),
        name="repack_tokens",
    )(place, arrived)


def hidden_kernel(parts, waited, place, x, dy, beside, *rest):
    weights = rest[:parts]
    mine, theirs, xs, dys, gates, ups, downs, sems = rest[parts + waited :]
    gate_rows, down_rows = HALF // parts, HID // parts
    cut = 2 * gate_rows
    copies = []
    for shift in range(CHIPS):
        chip = lax.rem(place[2] + shift, CHIPS)
        own = columns(chip * WIDE + place[0] * HALF)
        copies += [
            (x.at[:, own], xs.at[shift, :ROWS]),
            (dy.at[:, own], dys.at[shift, :ROWS]),
            (beside.at[chip, 0], xs.at[shift, ROWS:]),
            (beside.at[chip, 1], dys.at[shift, ROWS:]),
        ]
    for shift, ref in enumerate(weights):
        part = lax.rem(place[1] + shift, parts)
        to_gate = pl.ds(pl.multiple_of(part * gate_rows, gate_rows), gate_rows)
        to_down = pl.ds(pl.multiple_of(part * down_rows, down_rows), down_rows)
        copies += [
            (ref.at[:, pl.ds(0, gate_rows)], gates.at[:, to_gate]),
            (ref.at[:, pl.ds(gate_rows, gate_rows)], ups.at[:, to_gate]),
            (ref.at[:, pl.ds(cut, down_rows)], downs.at[:, 0, to_down]),
            (ref.at[:, pl.ds(cut + down_rows, down_rows)], downs.at[:, 1, to_down]),
        ]
    run_copies(copies, sems)
    gate = up = dh = 0.0
    for chip in range(CHIPS):
        a, b = xs[chip], dys[chip]
        gate += jnp.dot(a, gates[chip], preferred_element_type=F32)
        up += jnp.dot(a, ups[chip], preferred_element_type=F32)
        for h in range(2):
            dh += lax.dot_general(
                b[:, HID * h : HID * (h + 1)],
                downs[chip, h],
                (((1,), (1,)), ((), ())),
                preferred_element_type=F32,
            )
    for i, value in enumerate((gate, up, dh)):
        mine[i] = value[:ROWS]
        theirs[i] = value[ROWS:]


def hidden_sums(place, x, dy, beside, weights, after):
    out = jax.ShapeDtypeStruct((3, ROWS, HID), F32)
    return pl.pallas_call(
        functools.partial(hidden_kernel, len(weights), len(after)),
        out_shape=(out, out),
        in_specs=[SMEM] + [ANY] * (3 + len(weights) + len(after)),
        out_specs=(VMEM, VMEM),
        scratch_shapes=[
            pltpu.VMEM((CHIPS, 2 * ROWS, HALF), BF16),
            pltpu.VMEM((CHIPS, 2 * ROWS, HALF), BF16),
            pltpu.VMEM((CHIPS, HALF, HID), BF16),
            pltpu.VMEM((CHIPS, HALF, HID), BF16),
            pltpu.VMEM((CHIPS, 2, HID, HID), BF16),
            pltpu.SemaphoreType.DMA((4 * len(weights) + 16,)),
        ],
        compiler_params=pltpu.CompilerParams(vmem_limit_bytes=VMEM_LIMIT),
        cost_estimate=pl.CostEstimate(flops=6 * 256 * 2048 * 256, bytes_accessed=6 << 20, transcendentals=0),
        name="hidden_sums",
    )(place, x, dy, beside, *weights, *after)


def activation_kernel(mine_ref, arrived_ref, after, out, mine, arrived, sems):
    del after
    run_copies([(mine_ref, mine), (arrived_ref, arrived)], sems)
    gate = mine[0] + arrived[0]
    up = mine[1] + arrived[1]
    dh = mine[2] + arrived[2]
    sig = jax.nn.sigmoid(gate)
    active = gate * sig
    slope = sig * (1.0 + gate * (1.0 - sig))
    for i, value in enumerate((dh * up * slope, dh * active, active * up)):
        out[i] = value.astype(BF16)


def activation(mine, arrived, after):
    return pl.pallas_call(
        activation_kernel,
        out_shape=jax.ShapeDtypeStruct((3, ROWS, HID), BF16),
        in_specs=[ANY] * 3,
        out_specs=VMEM,
        scratch_shapes=[
            pltpu.VMEM((3, ROWS, HID), F32),
            pltpu.VMEM((3, ROWS, HID), F32),
            pltpu.SemaphoreType.DMA((2,)),
        ],
        cost_estimate=pl.CostEstimate(flops=20 * ROWS * HID, bytes_accessed=1 << 20, transcendentals=ROWS * HID),
        name="activation",
    )(mine, arrived, after)


def grads_kernel(place, arrived, swapped, *rest):
    acts, (gg, gu, gd, xs, dys, hs, sems) = rest[: 2 * CHIPS], rest[2 * CHIPS :]
    half = columns(place[0] * HALF)
    copies = []
    for i in range(CHIPS):
        near, far = pl.ds(i * ROWS, ROWS), pl.ds((CHIPS + i) * ROWS, ROWS)
        copies += [
            (arrived.at[i, 0, :, half], xs.at[near]),
            (arrived.at[i, 1, :, half], dys.at[near]),
            (swapped.at[i, 0], xs.at[far]),
            (swapped.at[i, 1], dys.at[far]),
        ]
    for shift in range(CHIPS):
        chip = lax.rem(place[2] + CHIPS - shift, CHIPS)
        near = pl.ds(pl.multiple_of(chip * ROWS, ROWS), ROWS)
        far = pl.ds(pl.multiple_of((CHIPS + chip) * ROWS, ROWS), ROWS)
        copies += [(acts[shift], hs.at[:, near]), (acts[CHIPS + shift], hs.at[:, far])]
    run_copies(copies, sems)
    tall = (((0,), (0,)), ((), ()))
    gg[0] = lax.dot_general(xs[...], hs[0], tall, preferred_element_type=F32).astype(BF16)
    gu[0] = lax.dot_general(xs[...], hs[1], tall, preferred_element_type=F32).astype(BF16)
    gd[0] = lax.dot_general(hs[2], dys[...], tall, preferred_element_type=F32).astype(BF16)


def grads(place, arrived, swapped, acts):
    tokens = 2 * CHIPS * ROWS
    return pl.pallas_call(
        grads_kernel,
        out_shape=(
            jax.ShapeDtypeStruct((1, HALF, HID), BF16),
            jax.ShapeDtypeStruct((1, HALF, HID), BF16),
            jax.ShapeDtypeStruct((1, HID, HALF), BF16),
        ),
        in_specs=[SMEM] + [ANY] * (2 + len(acts)),
        out_specs=(VMEM,) * 3,
        scratch_shapes=[
            pltpu.VMEM((tokens, HALF), BF16),
            pltpu.VMEM((tokens, HALF), BF16),
            pltpu.VMEM((3, tokens, HID), BF16),
            pltpu.SemaphoreType.DMA((24,)),
        ],
        compiler_params=pltpu.CompilerParams(vmem_limit_bytes=VMEM_LIMIT),
        cost_estimate=pl.CostEstimate(flops=6 * 1024 * 512 * 256, bytes_accessed=5 << 20, transcendentals=0),
        name="weight_grads",
    )(place, arrived, swapped, *acts)


def to_shift(value, shift):
    return lax.ppermute(value, "yh", [(i, (i + shift) % CHIPS) for i in range(CHIPS)])


def from_shift(value, shift):
    return lax.ppermute(value, "yh", [(i, (i - shift) % CHIPS) for i in range(CHIPS)])


def from_x(value, shift, size):
    return lax.ppermute(value, "x", [(i, (i - shift) % size) for i in range(size)])


def other_core(value):
    return lax.ppermute(value, "core", [(0, 1), (1, 0)])


def sum_over(total, names):
    for name in names:
        size = lax.axis_size(name)
        step = 1
        while step < size:
            total += lax.ppermute(total, name, [(i, i ^ step) for i in range(size)])
            step *= 2
    return total


def on_device(tokens, cotangent, w_gate, w_up, w_down, delta, anchor, momentum):
    x, dy = tokens[0], cotangent[0]
    place = jnp.stack([lax.axis_index(name) for name in ("core", "x", "yh")]).astype(jnp.int32)
    parts = lax.axis_size("x")

    share = own_share(place, w_gate, w_up, w_down, parts)
    shares = {shift: from_shift(share, shift) for shift in (1, 2, 3)}
    shares = jnp.stack([share] + [shares[shift] for shift in (1, 2, 3)])
    weights = [shares] + [from_x(shares, shift, parts) for shift in range(1, parts)]

    partial = sum_over(delta[0], ("yl", "x"))
    packed, beside = pack(place, x, dy, shares, partial)
    arrived = lax.all_to_all(packed, "yh", 0, 0, tiled=True)
    beside = other_core(beside)
    swapped = other_core(repack(place, arrived))

    pseudo = sum_over(partial, ("z",)) / lax.axis_size(("yl", "x", "z"))
    new_momentum = 0.9 * momentum + pseudo
    new_anchor = anchor - 0.7 * (pseudo + 0.9 * new_momentum)

    mine, theirs = hidden_sums(place, x, dy, beside, weights, ())
    acts = activation(mine, other_core(theirs), new_anchor)
    acts = [acts] + [to_shift(acts, shift) for shift in (1, 2, 3)]
    acts += [other_core(value) for value in acts]
    grad_gate, grad_up, grad_down = grads(place, arrived, swapped, acts)
    return grad_gate, grad_up, grad_down, new_anchor, new_momentum


def solution(mesh):
    fine = Mesh(mesh.devices.reshape(4, 2, 2, 4, 8), ("yh", "core", "yl", "x", "z"))
    fsdp, replica = ("yh", "core"), ("yl", "x", "z")
    placed = (
        P(replica, fsdp, None),
        P(replica, fsdp, None),
        P(fsdp, None),
        P(fsdp, None),
        P(None, fsdp),
        P(replica, fsdp, None),
        P(fsdp, None),
        P(fsdp, None),
    )
    return jax.shard_map(
        on_device,
        mesh=fine,
        in_specs=placed,
        out_specs=(
            P(replica, fsdp, None),
            P(replica, fsdp, None),
            P(replica, None, fsdp),
            P(fsdp, None),
            P(fsdp, None),
        ),
        check_vma=False,
    )
```

```python
import functools

import jax
import jax.numpy as jnp
from jax import lax
from jax.experimental import pallas as pl
from jax.experimental.pallas import tpu as pltpu
from jax.sharding import Mesh
from jax.sharding import PartitionSpec as P

CHIPS = 4
ROWS = 128
WIDE = 1024
HALF = 512
HID = 256
DEAR = 100
VMEM_LIMIT = 48 * 1024 * 1024

F32 = jnp.float32
BF16 = jnp.bfloat16
ANY = pl.BlockSpec(memory_space=pl.ANY)
VMEM = pl.BlockSpec(memory_space=pltpu.VMEM)
SMEM = pl.BlockSpec(memory_space=pltpu.SMEM)


def run_copies(copies, sems):
    started = [pltpu.make_async_copy(src, dst, sems.at[i]) for i, (src, dst) in enumerate(copies)]
    for copy in started:
        copy.start()
    for copy in started:
        copy.wait()


def columns(base):
    return pl.ds(pl.multiple_of(base, HALF), HALF)


def wide_columns(chip):
    return pl.ds(pl.multiple_of(chip * WIDE, WIDE), WIDE)


def share_kernel(parts, place, gate, up, down, out, sems):
    gate_rows, down_rows = HALF // parts, HID // parts
    cut = 2 * gate_rows
    at_gate = pl.ds(pl.multiple_of(place[1] * gate_rows, gate_rows), gate_rows)
    at_down = pl.ds(pl.multiple_of(place[1] * down_rows, down_rows), down_rows)
    copies = [
        (gate.at[at_gate], out.at[pl.ds(0, gate_rows)]),
        (up.at[at_gate], out.at[pl.ds(gate_rows, gate_rows)]),
        (down.at[at_down, :HID], out.at[pl.ds(cut, down_rows)]),
        (down.at[at_down, HID:], out.at[pl.ds(cut + down_rows, down_rows)]),
    ]
    run_copies(copies, sems)


def own_share(place, gate, up, down, parts):
    return pl.pallas_call(
        functools.partial(share_kernel, parts),
        out_shape=jax.ShapeDtypeStruct((2 * (HALF + HID) // parts, HID), BF16),
        in_specs=[SMEM, ANY, ANY, ANY],
        out_specs=VMEM,
        scratch_shapes=[pltpu.SemaphoreType.DMA((4,))],
        cost_estimate=pl.CostEstimate(flops=0, bytes_accessed=1 << 18, transcendentals=0),
        name="weight_share",
    )(place, gate, up, down)


def beside_kernel(place, x, dy, after, out, sems):
    del after
    copies = []
    for i in range(CHIPS):
        other = columns(i * WIDE + (1 - place[0]) * HALF)
        copies += [(x.at[:, other], out.at[i, 0]), (dy.at[:, other], out.at[i, 1])]
    run_copies(copies, sems)


def for_beside(place, x, dy, after):
    return pl.pallas_call(
        beside_kernel,
        out_shape=jax.ShapeDtypeStruct((CHIPS, 2, ROWS, HALF), BF16),
        in_specs=[SMEM] + [ANY] * 3,
        out_specs=VMEM,
        scratch_shapes=[pltpu.SemaphoreType.DMA((8,))],
        compiler_params=pltpu.CompilerParams(vmem_limit_bytes=VMEM_LIMIT),
        cost_estimate=pl.CostEstimate(flops=0, bytes_accessed=2 << 20, transcendentals=0),
        name="tokens_beside",
    )(place, x, dy, after)


def pack_kernel(waited, place, x, dy, *rest):
    ahead, back, sems = rest[waited:]
    chip = place[2]
    near, far, last = (wide_columns(lax.rem(chip + shift, CHIPS)) for shift in (1, 2, 3))
    copies = [
        (x.at[:, near], ahead.at[0]),
        (dy.at[:, near], ahead.at[1]),
        (x.at[:, far], ahead.at[2]),
        (x.at[:, last], back.at[0]),
        (dy.at[:, last], back.at[1]),
        (dy.at[:, far], back.at[2]),
    ]
    run_copies(copies, sems)


def pack(place, x, dy, after):
    wide = jax.ShapeDtypeStruct((3, ROWS, WIDE), BF16)
    return pl.pallas_call(
        functools.partial(pack_kernel, len(after)),
        out_shape=(wide, wide),
        in_specs=[SMEM] + [ANY] * (2 + len(after)),
        out_specs=(VMEM, VMEM),
        scratch_shapes=[pltpu.SemaphoreType.DMA((6,))],
        compiler_params=pltpu.CompilerParams(vmem_limit_bytes=VMEM_LIMIT),
        cost_estimate=pl.CostEstimate(flops=0, bytes_accessed=4 << 20, transcendentals=0),
        name="pack_tokens",
    )(place, x, dy, *after)


def onward_kernel(ahead, back, far_x, far_dy, sems):
    run_copies([(ahead.at[2], far_x.at[0]), (back.at[2], far_dy.at[0])], sems)


def onward(ahead, back):
    one = jax.ShapeDtypeStruct((1, ROWS, WIDE), BF16)
    return pl.pallas_call(
        onward_kernel,
        out_shape=(one, one),
        in_specs=[ANY, ANY],
        out_specs=(VMEM, VMEM),
        scratch_shapes=[pltpu.SemaphoreType.DMA((2,))],
        cost_estimate=pl.CostEstimate(flops=0, bytes_accessed=DEAR << 20, transcendentals=0),
        name="onward",
    )(ahead, back)


def repack_kernel(place, ahead, back, far_x, far_dy, out, sems):
    other = columns((1 - place[0]) * HALF)
    copies = []
    for i, (a, b) in enumerate(((ahead.at[0], ahead.at[1]), (far_x.at[0], far_dy.at[0]), (back.at[0], back.at[1]))):
        copies += [(a.at[:, other], out.at[i, 0]), (b.at[:, other], out.at[i, 1])]
    run_copies(copies, sems)


def repack(place, arrived):
    return pl.pallas_call(
        repack_kernel,
        out_shape=jax.ShapeDtypeStruct((CHIPS - 1, 2, ROWS, HALF), BF16),
        in_specs=[SMEM] + [ANY] * 4,
        out_specs=VMEM,
        scratch_shapes=[pltpu.SemaphoreType.DMA((6,))],
        compiler_params=pltpu.CompilerParams(vmem_limit_bytes=VMEM_LIMIT),
        cost_estimate=pl.CostEstimate(flops=0, bytes_accessed=DEAR * 2 << 20, transcendentals=0),
        name="repack_tokens",
    )(place, *arrived)


def staged_kernel(delta, after, out, sem):
    del after
    run_copies([(delta, out)], sem)


def staged(delta, after):
    return pl.pallas_call(
        staged_kernel,
        out_shape=jax.ShapeDtypeStruct(delta.shape, delta.dtype),
        in_specs=[ANY, ANY],
        out_specs=VMEM,
        scratch_shapes=[pltpu.SemaphoreType.DMA((1,))],
        cost_estimate=pl.CostEstimate(flops=0, bytes_accessed=1 << 19, transcendentals=0),
        name="delta_staged",
    )(delta, after)


def hidden_kernel(parts, waited, place, x, dy, beside, *rest):
    weights = rest[:parts]
    mine, theirs, xs, dys, gates, ups, downs, sems = rest[parts + waited :]
    gate_rows, down_rows = HALF // parts, HID // parts
    cut = 2 * gate_rows
    copies = []
    for shift in range(CHIPS):
        chip = lax.rem(place[2] + shift, CHIPS)
        own = columns(chip * WIDE + place[0] * HALF)
        copies += [
            (x.at[:, own], xs.at[shift, :ROWS]),
            (dy.at[:, own], dys.at[shift, :ROWS]),
            (beside.at[chip, 0], xs.at[shift, ROWS:]),
            (beside.at[chip, 1], dys.at[shift, ROWS:]),
        ]
    for shift, ref in enumerate(weights):
        part = lax.rem(place[1] + shift, parts)
        to_gate = pl.ds(pl.multiple_of(part * gate_rows, gate_rows), gate_rows)
        to_down = pl.ds(pl.multiple_of(part * down_rows, down_rows), down_rows)
        copies += [
            (ref.at[:, pl.ds(0, gate_rows)], gates.at[:, to_gate]),
            (ref.at[:, pl.ds(gate_rows, gate_rows)], ups.at[:, to_gate]),
            (ref.at[:, pl.ds(cut, down_rows)], downs.at[:, 0, to_down]),
            (ref.at[:, pl.ds(cut + down_rows, down_rows)], downs.at[:, 1, to_down]),
        ]
    run_copies(copies, sems)
    gate = up = dh = 0.0
    for chip in range(CHIPS):
        a, b = xs[chip], dys[chip]
        gate += jnp.dot(a, gates[chip], preferred_element_type=F32)
        up += jnp.dot(a, ups[chip], preferred_element_type=F32)
        for h in range(2):
            dh += lax.dot_general(
                b[:, HID * h : HID * (h + 1)],
                downs[chip, h],
                (((1,), (1,)), ((), ())),
                preferred_element_type=F32,
            )
    for i, value in enumerate((gate, up, dh)):
        mine[i] = value[:ROWS]
        theirs[i] = value[ROWS:]


def hidden_sums(place, x, dy, beside, weights, after):
    out = jax.ShapeDtypeStruct((3, ROWS, HID), F32)
    return pl.pallas_call(
        functools.partial(hidden_kernel, len(weights), len(after)),
        out_shape=(out, out),
        in_specs=[SMEM] + [ANY] * (3 + len(weights) + len(after)),
        out_specs=(VMEM, VMEM),
        scratch_shapes=[
            pltpu.VMEM((CHIPS, 2 * ROWS, HALF), BF16),
            pltpu.VMEM((CHIPS, 2 * ROWS, HALF), BF16),
            pltpu.VMEM((CHIPS, HALF, HID), BF16),
            pltpu.VMEM((CHIPS, HALF, HID), BF16),
            pltpu.VMEM((CHIPS, 2, HID, HID), BF16),
            pltpu.SemaphoreType.DMA((4 * len(weights) + 16,)),
        ],
        compiler_params=pltpu.CompilerParams(vmem_limit_bytes=VMEM_LIMIT),
        cost_estimate=pl.CostEstimate(flops=6 * 256 * 2048 * 256, bytes_accessed=6 << 20, transcendentals=0),
        name="hidden_sums",
    )(place, x, dy, beside, *weights, *after)


def activation_kernel(mine_ref, arrived_ref, after, out, mine, arrived, sems):
    del after
    run_copies([(mine_ref, mine), (arrived_ref, arrived)], sems)
    gate = mine[0] + arrived[0]
    up = mine[1] + arrived[1]
    dh = mine[2] + arrived[2]
    sig = jax.nn.sigmoid(gate)
    active = gate * sig
    slope = sig * (1.0 + gate * (1.0 - sig))
    for i, value in enumerate((dh * up * slope, dh * active, active * up)):
        for chip in range(CHIPS):
            out[chip, i] = value.astype(BF16)


def activation(mine, arrived, after):
    return pl.pallas_call(
        activation_kernel,
        out_shape=jax.ShapeDtypeStruct((CHIPS, 3, ROWS, HID), BF16),
        in_specs=[ANY] * 3,
        out_specs=VMEM,
        scratch_shapes=[
            pltpu.VMEM((3, ROWS, HID), F32),
            pltpu.VMEM((3, ROWS, HID), F32),
            pltpu.SemaphoreType.DMA((2,)),
        ],
        cost_estimate=pl.CostEstimate(flops=20 * ROWS * HID, bytes_accessed=1 << 20, transcendentals=ROWS * HID),
        name="activation",
    )(mine, arrived, after)


def grads_kernel(place, x, dy, beside, ahead, back, far_x, far_dy, swapped, *rest):
    acts, (gg, gu, gd, xs, dys, hs, sems) = rest[:2], rest[2:]
    core, chip = place[0], place[2]
    half, own = columns(core * HALF), columns(chip * WIDE + core * HALF)
    here = [(x.at[:, own], dy.at[:, own])]
    here += [
        (a.at[:, half], b.at[:, half])
        for a, b in ((ahead.at[0], ahead.at[1]), (far_x.at[0], far_dy.at[0]), (back.at[0], back.at[1]))
    ]
    there = [(beside.at[chip, 0], beside.at[chip, 1])]
    there += [(swapped.at[i, 0], swapped.at[i, 1]) for i in range(CHIPS - 1)]
    copies = []
    for i, (a, b) in enumerate(here + there):
        rows = pl.ds(i * ROWS, ROWS)
        source = lax.rem(chip + 2 * CHIPS - i, CHIPS)
        copies += [(a, xs.at[rows]), (b, dys.at[rows]), (acts[i // CHIPS].at[source], hs.at[:, rows])]
    run_copies(copies, sems)
    tall = (((0,), (0,)), ((), ()))
    gg[0] = lax.dot_general(xs[...], hs[0], tall, preferred_element_type=F32).astype(BF16)
    gu[0] = lax.dot_general(xs[...], hs[1], tall, preferred_element_type=F32).astype(BF16)
    gd[0] = lax.dot_general(hs[2], dys[...], tall, preferred_element_type=F32).astype(BF16)


def grads(place, x, dy, beside, arrived, swapped, acts):
    tokens = 2 * CHIPS * ROWS
    return pl.pallas_call(
        grads_kernel,
        out_shape=(
            jax.ShapeDtypeStruct((1, HALF, HID), BF16),
            jax.ShapeDtypeStruct((1, HALF, HID), BF16),
            jax.ShapeDtypeStruct((1, HID, HALF), BF16),
        ),
        in_specs=[SMEM] + [ANY] * (8 + len(acts)),
        out_specs=(VMEM,) * 3,
        scratch_shapes=[
            pltpu.VMEM((tokens, HALF), BF16),
            pltpu.VMEM((tokens, HALF), BF16),
            pltpu.VMEM((3, tokens, HID), BF16),
            pltpu.SemaphoreType.DMA((24,)),
        ],
        compiler_params=pltpu.CompilerParams(vmem_limit_bytes=VMEM_LIMIT),
        cost_estimate=pl.CostEstimate(flops=6 * 1024 * 512 * 256, bytes_accessed=5 << 20, transcendentals=0),
        name="weight_grads",
    )(place, x, dy, beside, *arrived, swapped, *acts)


def to_shift(value, shift):
    return lax.ppermute(value, "yh", [(i, (i + shift) % CHIPS) for i in range(CHIPS)])


def from_shift(value, shift):
    return lax.ppermute(value, "yh", [(i, (i - shift) % CHIPS) for i in range(CHIPS)])


def from_x(value, shift, size):
    return lax.ppermute(value, "x", [(i, (i - shift) % size) for i in range(size)])


def other_core(value):
    return lax.ppermute(value, "core", [(0, 1), (1, 0)])


def share_of_sum(delta):
    everyone = ("yl", "x", "z")
    count = lax.axis_size(everyone)
    rows, cols = delta.shape
    tiles = delta.reshape(rows // 8, 8, cols // 128, 128).transpose(0, 2, 1, 3).reshape(count, 8, 128)
    return jnp.sum(lax.all_to_all(tiles, everyone, 0, 0, tiled=True), axis=0, keepdims=True)


def whole_mean(part, shape):
    everyone = ("yl", "x", "z")
    count = lax.axis_size(everyone)
    rows, cols = shape
    whole = lax.all_to_all(jnp.broadcast_to(part / count, (count, 8, 128)), everyone, 0, 0, tiled=True)
    return whole.reshape(rows // 8, cols // 128, 8, 128).transpose(0, 2, 1, 3).reshape(rows, cols)


def on_device(tokens, cotangent, w_gate, w_up, w_down, delta, anchor, momentum):
    x, dy = tokens[0], cotangent[0]
    place = jnp.stack([lax.axis_index(name) for name in ("core", "x", "yh")]).astype(jnp.int32)
    parts = lax.axis_size("x")

    share = own_share(place, w_gate, w_up, w_down, parts)
    shares = {shift: from_shift(share, shift) for shift in (1, 2, 3)}
    shares = jnp.stack([share] + [shares[shift] for shift in (1, 2, 3)])
    weights = [shares] + [from_x(shares, shift, parts) for shift in range(1, parts)]

    beside = other_core(for_beside(place, x, dy, share))
    part = share_of_sum(staged(delta[0], beside))
    ahead, back = pack(place, x, dy, (shares, beside))
    ahead, back = to_shift(ahead, 1), to_shift(back, 3)
    far_x, far_dy = onward(ahead, back)
    arrived = [ahead, back, to_shift(far_x, 1), to_shift(far_dy, 3)]
    repacked = repack(place, arrived)
    swapped = other_core(repacked)

    pseudo = whole_mean(part, anchor.shape)
    new_momentum = 0.9 * momentum + pseudo
    new_anchor = anchor - 0.7 * (pseudo + 0.9 * new_momentum)

    mine, theirs = hidden_sums(place, x, dy, beside, weights, (repacked,))
    acts = activation(mine, other_core(theirs), new_anchor)
    acts = lax.all_to_all(acts, "yh", 0, 0, tiled=True)
    acts = (acts, other_core(acts))
    grad_gate, grad_up, grad_down = grads(place, x, dy, beside, arrived, swapped, acts)
    return grad_gate, grad_up, grad_down, new_anchor, new_momentum


def solution(mesh):
    fine = Mesh(mesh.devices.reshape(4, 2, 2, 4, 8), ("yh", "core", "yl", "x", "z"))
    fsdp, replica = ("yh", "core"), ("yl", "x", "z")
    placed = (
        P(replica, fsdp, None),
        P(replica, fsdp, None),
        P(fsdp, None),
        P(fsdp, None),
        P(None, fsdp),
        P(replica, fsdp, None),
        P(fsdp, None),
        P(fsdp, None),
    )
    return jax.shard_map(
        on_device,
        mesh=fine,
        in_specs=placed,
        out_specs=(
            P(replica, fsdp, None),
            P(replica, fsdp, None),
            P(replica, None, fsdp),
            P(fsdp, None),
            P(fsdp, None),
        ),
        check_vma=False,
    )
```

```python
import functools

import jax
import jax.numpy as jnp
from jax import lax
from jax.experimental import pallas as pl
from jax.experimental.pallas import tpu as pltpu
from jax.sharding import Mesh
from jax.sharding import PartitionSpec as P

CHIPS = 4
ROWS = 128
WIDE = 1024
HALF = 512
HID = 256
DEAR = 100
VMEM_LIMIT = 63 * 1024 * 1024

F32 = jnp.float32
BF16 = jnp.bfloat16
ANY = pl.BlockSpec(memory_space=pl.ANY)
VMEM = pl.BlockSpec(memory_space=pltpu.VMEM)
SMEM = pl.BlockSpec(memory_space=pltpu.SMEM)


def run_copies(copies, sems):
    started = [pltpu.make_async_copy(src, dst, sems.at[i]) for i, (src, dst) in enumerate(copies)]
    for copy in started:
        copy.start()
    for copy in started:
        copy.wait()


def columns(base):
    return pl.ds(pl.multiple_of(base, HALF), HALF)


def wide_columns(chip):
    return pl.ds(pl.multiple_of(chip * WIDE, WIDE), WIDE)


def share_kernel(parts, place, gate, up, down, out, sems):
    gate_rows, down_rows = HALF // parts, HID // parts
    cut = 2 * gate_rows
    at_gate = pl.ds(pl.multiple_of(place[1] * gate_rows, gate_rows), gate_rows)
    at_down = pl.ds(pl.multiple_of(place[1] * down_rows, down_rows), down_rows)
    copies = [
        (gate.at[at_gate], out.at[pl.ds(0, gate_rows)]),
        (up.at[at_gate], out.at[pl.ds(gate_rows, gate_rows)]),
        (down.at[at_down, :HID], out.at[pl.ds(cut, down_rows)]),
        (down.at[at_down, HID:], out.at[pl.ds(cut + down_rows, down_rows)]),
    ]
    run_copies(copies, sems)


def own_share(place, gate, up, down, parts):
    return pl.pallas_call(
        functools.partial(share_kernel, parts),
        out_shape=jax.ShapeDtypeStruct((2 * (HALF + HID) // parts, HID), BF16),
        in_specs=[SMEM, ANY, ANY, ANY],
        out_specs=VMEM,
        scratch_shapes=[pltpu.SemaphoreType.DMA((4,))],
        compiler_params=pltpu.CompilerParams(vmem_limit_bytes=VMEM_LIMIT),
        cost_estimate=pl.CostEstimate(flops=0, bytes_accessed=1 << 18, transcendentals=0),
        name="weight_share",
    )(place, gate, up, down)


def beside_kernel(place, x, dy, after, out, sems):
    del after
    copies = []
    for i in range(CHIPS):
        other = columns(i * WIDE + (1 - place[0]) * HALF)
        copies += [(x.at[:, other], out.at[i, 0]), (dy.at[:, other], out.at[i, 1])]
    run_copies(copies, sems)


def for_beside(place, x, dy, after):
    return pl.pallas_call(
        beside_kernel,
        out_shape=jax.ShapeDtypeStruct((CHIPS, 2, ROWS, HALF), BF16),
        in_specs=[SMEM] + [ANY] * 3,
        out_specs=VMEM,
        scratch_shapes=[pltpu.SemaphoreType.DMA((8,))],
        compiler_params=pltpu.CompilerParams(vmem_limit_bytes=VMEM_LIMIT),
        cost_estimate=pl.CostEstimate(flops=0, bytes_accessed=2 << 20, transcendentals=0),
        name="tokens_beside",
    )(place, x, dy, after)


def pack_kernel(waited, place, x, dy, *rest):
    ahead, back, sems = rest[waited:]
    chip = place[2]
    near, far, last = (wide_columns(lax.rem(chip + shift, CHIPS)) for shift in (1, 2, 3))
    copies = [
        (x.at[:, near], ahead.at[0]),
        (dy.at[:, near], ahead.at[1]),
        (x.at[:, far], ahead.at[2]),
        (x.at[:, last], back.at[0]),
        (dy.at[:, last], back.at[1]),
        (dy.at[:, far], back.at[2]),
    ]
    run_copies(copies, sems)


def pack(place, x, dy, after):
    wide = jax.ShapeDtypeStruct((3, ROWS, WIDE), BF16)
    return pl.pallas_call(
        functools.partial(pack_kernel, len(after)),
        out_shape=(wide, wide),
        in_specs=[SMEM] + [ANY] * (2 + len(after)),
        out_specs=(VMEM, VMEM),
        scratch_shapes=[pltpu.SemaphoreType.DMA((6,))],
        compiler_params=pltpu.CompilerParams(vmem_limit_bytes=VMEM_LIMIT),
        cost_estimate=pl.CostEstimate(flops=0, bytes_accessed=4 << 20, transcendentals=0),
        name="pack_tokens",
    )(place, x, dy, *after)


def onward_kernel(ahead, back, far_x, far_dy, sems):
    run_copies([(ahead.at[2], far_x.at[0]), (back.at[2], far_dy.at[0])], sems)


def onward(ahead, back):
    one = jax.ShapeDtypeStruct((1, ROWS, WIDE), BF16)
    return pl.pallas_call(
        onward_kernel,
        out_shape=(one, one),
        in_specs=[ANY, ANY],
        out_specs=(VMEM, VMEM),
        scratch_shapes=[pltpu.SemaphoreType.DMA((2,))],
        compiler_params=pltpu.CompilerParams(vmem_limit_bytes=VMEM_LIMIT),
        cost_estimate=pl.CostEstimate(flops=0, bytes_accessed=DEAR << 20, transcendentals=0),
        name="onward",
    )(ahead, back)


def repack_kernel(place, ahead, back, far_x, far_dy, out, sems):
    other = columns((1 - place[0]) * HALF)
    copies = []
    for i, (a, b) in enumerate(((ahead.at[0], ahead.at[1]), (far_x.at[0], far_dy.at[0]), (back.at[0], back.at[1]))):
        copies += [(a.at[:, other], out.at[i, 0]), (b.at[:, other], out.at[i, 1])]
    run_copies(copies, sems)


def repack(place, arrived):
    return pl.pallas_call(
        repack_kernel,
        out_shape=jax.ShapeDtypeStruct((CHIPS - 1, 2, ROWS, HALF), BF16),
        in_specs=[SMEM] + [ANY] * 4,
        out_specs=VMEM,
        scratch_shapes=[pltpu.SemaphoreType.DMA((6,))],
        compiler_params=pltpu.CompilerParams(vmem_limit_bytes=VMEM_LIMIT),
        cost_estimate=pl.CostEstimate(flops=0, bytes_accessed=DEAR * 2 << 20, transcendentals=0),
        name="repack_tokens",
    )(place, *arrived)


def staged_kernel(delta, after, out, sem):
    del after
    run_copies([(delta, out)], sem)


def staged(delta, after):
    return pl.pallas_call(
        staged_kernel,
        out_shape=jax.ShapeDtypeStruct(delta.shape, delta.dtype),
        in_specs=[ANY, ANY],
        out_specs=VMEM,
        scratch_shapes=[pltpu.SemaphoreType.DMA((1,))],
        compiler_params=pltpu.CompilerParams(vmem_limit_bytes=VMEM_LIMIT),
        cost_estimate=pl.CostEstimate(flops=0, bytes_accessed=1 << 19, transcendentals=0),
        name="delta_staged",
    )(delta, after)


def hidden_kernel(parts, waited, place, x, dy, beside, *rest):
    weights = rest[:parts]
    mine, theirs, xs, dys, gates, ups, downs, sems = rest[parts + waited :]
    gate_rows, down_rows = HALF // parts, HID // parts
    cut = 2 * gate_rows
    copies = []
    for shift in range(CHIPS):
        chip = lax.rem(place[2] + shift, CHIPS)
        own = columns(chip * WIDE + place[0] * HALF)
        copies += [
            (x.at[:, own], xs.at[shift, :ROWS]),
            (dy.at[:, own], dys.at[shift, :ROWS]),
            (beside.at[chip, 0], xs.at[shift, ROWS:]),
            (beside.at[chip, 1], dys.at[shift, ROWS:]),
        ]
    for shift, ref in enumerate(weights):
        part = lax.rem(place[1] + shift, parts)
        to_gate = pl.ds(pl.multiple_of(part * gate_rows, gate_rows), gate_rows)
        to_down = pl.ds(pl.multiple_of(part * down_rows, down_rows), down_rows)
        copies += [
            (ref.at[:, pl.ds(0, gate_rows)], gates.at[:, to_gate]),
            (ref.at[:, pl.ds(gate_rows, gate_rows)], ups.at[:, to_gate]),
            (ref.at[:, pl.ds(cut, down_rows)], downs.at[:, 0, to_down]),
            (ref.at[:, pl.ds(cut + down_rows, down_rows)], downs.at[:, 1, to_down]),
        ]
    run_copies(copies, sems)
    gate = up = dh = 0.0
    for chip in range(CHIPS):
        a, b = xs[chip], dys[chip]
        gate += jnp.dot(a, gates[chip], preferred_element_type=F32)
        up += jnp.dot(a, ups[chip], preferred_element_type=F32)
        for h in range(2):
            dh += lax.dot_general(
                b[:, HID * h : HID * (h + 1)],
                downs[chip, h],
                (((1,), (1,)), ((), ())),
                preferred_element_type=F32,
            )
    for i, value in enumerate((gate, up, dh)):
        mine[i] = value[:ROWS]
        theirs[i] = value[ROWS:]


def hidden_sums(place, x, dy, beside, weights, after):
    out = jax.ShapeDtypeStruct((3, ROWS, HID), F32)
    return pl.pallas_call(
        functools.partial(hidden_kernel, len(weights), len(after)),
        out_shape=(out, out),
        in_specs=[SMEM] + [ANY] * (3 + len(weights) + len(after)),
        out_specs=(VMEM, VMEM),
        scratch_shapes=[
            pltpu.VMEM((CHIPS, 2 * ROWS, HALF), BF16),
            pltpu.VMEM((CHIPS, 2 * ROWS, HALF), BF16),
            pltpu.VMEM((CHIPS, HALF, HID), BF16),
            pltpu.VMEM((CHIPS, HALF, HID), BF16),
            pltpu.VMEM((CHIPS, 2, HID, HID), BF16),
            pltpu.SemaphoreType.DMA((4 * len(weights) + 16,)),
        ],
        compiler_params=pltpu.CompilerParams(vmem_limit_bytes=VMEM_LIMIT),
        cost_estimate=pl.CostEstimate(flops=6 * 256 * 2048 * 256, bytes_accessed=6 << 20, transcendentals=0),
        name="hidden_sums",
    )(place, x, dy, beside, *weights, *after)


def activation_kernel(mine_ref, arrived_ref, after, out, mine, arrived, sems):
    del after
    run_copies([(mine_ref, mine), (arrived_ref, arrived)], sems)
    gate = mine[0] + arrived[0]
    up = mine[1] + arrived[1]
    dh = mine[2] + arrived[2]
    sig = jax.nn.sigmoid(gate)
    active = gate * sig
    slope = sig * (1.0 + gate * (1.0 - sig))
    for i, value in enumerate((dh * up * slope, dh * active, active * up)):
        for chip in range(CHIPS):
            out[chip, i] = value.astype(BF16)


def activation(mine, arrived, after):
    return pl.pallas_call(
        activation_kernel,
        out_shape=jax.ShapeDtypeStruct((CHIPS, 3, ROWS, HID), BF16),
        in_specs=[ANY] * 3,
        out_specs=VMEM,
        scratch_shapes=[
            pltpu.VMEM((3, ROWS, HID), F32),
            pltpu.VMEM((3, ROWS, HID), F32),
            pltpu.SemaphoreType.DMA((2,)),
        ],
        compiler_params=pltpu.CompilerParams(vmem_limit_bytes=VMEM_LIMIT),
        cost_estimate=pl.CostEstimate(flops=20 * ROWS * HID, bytes_accessed=1 << 20, transcendentals=ROWS * HID),
        name="activation",
    )(mine, arrived, after)


def grads_kernel(place, x, dy, beside, ahead, back, far_x, far_dy, swapped, *rest):
    acts, (gg, gu, gd, xs, dys, hs, sems) = rest[:2], rest[2:]
    core, chip = place[0], place[2]
    half, own = columns(core * HALF), columns(chip * WIDE + core * HALF)
    here = [(x.at[:, own], dy.at[:, own])]
    here += [
        (a.at[:, half], b.at[:, half])
        for a, b in ((ahead.at[0], ahead.at[1]), (far_x.at[0], far_dy.at[0]), (back.at[0], back.at[1]))
    ]
    there = [(beside.at[chip, 0], beside.at[chip, 1])]
    there += [(swapped.at[i, 0], swapped.at[i, 1]) for i in range(CHIPS - 1)]
    copies = []
    for i, (a, b) in enumerate(here + there):
        rows = pl.ds(i * ROWS, ROWS)
        source = lax.rem(chip + 2 * CHIPS - i, CHIPS)
        copies += [(a, xs.at[rows]), (b, dys.at[rows]), (acts[i // CHIPS].at[source], hs.at[:, rows])]
    run_copies(copies, sems)
    tall = (((0,), (0,)), ((), ()))
    gg[0] = lax.dot_general(xs[...], hs[0], tall, preferred_element_type=F32).astype(BF16)
    gu[0] = lax.dot_general(xs[...], hs[1], tall, preferred_element_type=F32).astype(BF16)
    gd[0] = lax.dot_general(hs[2], dys[...], tall, preferred_element_type=F32).astype(BF16)


def grads(place, x, dy, beside, arrived, swapped, acts):
    tokens = 2 * CHIPS * ROWS
    return pl.pallas_call(
        grads_kernel,
        out_shape=(
            jax.ShapeDtypeStruct((1, HALF, HID), BF16),
            jax.ShapeDtypeStruct((1, HALF, HID), BF16),
            jax.ShapeDtypeStruct((1, HID, HALF), BF16),
        ),
        in_specs=[SMEM] + [ANY] * (8 + len(acts)),
        out_specs=(VMEM,) * 3,
        scratch_shapes=[
            pltpu.VMEM((tokens, HALF), BF16),
            pltpu.VMEM((tokens, HALF), BF16),
            pltpu.VMEM((3, tokens, HID), BF16),
            pltpu.SemaphoreType.DMA((24,)),
        ],
        compiler_params=pltpu.CompilerParams(vmem_limit_bytes=VMEM_LIMIT),
        cost_estimate=pl.CostEstimate(flops=6 * 1024 * 512 * 256, bytes_accessed=5 << 20, transcendentals=0),
        name="weight_grads",
    )(place, x, dy, beside, *arrived, swapped, *acts)


def to_shift(value, shift):
    return lax.ppermute(value, "yh", [(i, (i + shift) % CHIPS) for i in range(CHIPS)])


def from_shift(value, shift):
    return lax.ppermute(value, "yh", [(i, (i - shift) % CHIPS) for i in range(CHIPS)])


def from_x(value, shift, size):
    return lax.ppermute(value, "x", [(i, (i - shift) % size) for i in range(size)])


def other_core(value):
    return lax.ppermute(value, "core", [(0, 1), (1, 0)])


def share_of_sum(delta):
    everyone = ("yl", "x", "z")
    count = lax.axis_size(everyone)
    rows, cols = delta.shape
    tiles = delta.reshape(rows // 8, 8, cols // 128, 128).transpose(0, 2, 1, 3).reshape(count, 8, 128)
    return jnp.sum(lax.all_to_all(tiles, everyone, 0, 0, tiled=True), axis=0, keepdims=True)


def whole_mean(part, shape):
    everyone = ("yl", "x", "z")
    count = lax.axis_size(everyone)
    rows, cols = shape
    whole = lax.all_to_all(jnp.broadcast_to(part / count, (count, 8, 128)), everyone, 0, 0, tiled=True)
    return whole.reshape(rows // 8, cols // 128, 8, 128).transpose(0, 2, 1, 3).reshape(rows, cols)


def on_device(tokens, cotangent, w_gate, w_up, w_down, delta, anchor, momentum):
    x, dy = tokens[0], cotangent[0]
    place = jnp.stack([lax.axis_index(name) for name in ("core", "x", "yh")]).astype(jnp.int32)
    parts = lax.axis_size("x")

    share = own_share(place, w_gate, w_up, w_down, parts)
    shares = {shift: from_shift(share, shift) for shift in (1, 2, 3)}
    shares = jnp.stack([share] + [shares[shift] for shift in (1, 2, 3)])
    weights = [shares] + [from_x(shares, shift, parts) for shift in range(1, parts)]

    beside = other_core(for_beside(place, x, dy, share))
    part = share_of_sum(staged(delta[0], beside))
    ahead, back = pack(place, x, dy, (shares, beside))
    ahead, back = to_shift(ahead, 1), to_shift(back, 3)
    far_x, far_dy = onward(ahead, back)
    far_x, far_dy = to_shift(far_x, 1), to_shift(far_dy, 3)
    arrived = [ahead, back, far_x, far_dy]
    repacked = repack(place, arrived)
    swapped = other_core(repacked)

    pseudo = whole_mean(part, anchor.shape)
    new_momentum = 0.9 * momentum + pseudo
    new_anchor = anchor - 0.7 * (pseudo + 0.9 * new_momentum)

    mine, theirs = hidden_sums(place, x, dy, beside, weights, (far_x, far_dy))
    acts = activation(mine, other_core(theirs), new_anchor)
    acts = lax.all_to_all(acts, "yh", 0, 0, tiled=True)
    acts = (acts, other_core(acts))
    grad_gate, grad_up, grad_down = grads(place, x, dy, beside, arrived, swapped, acts)
    return grad_gate, grad_up, grad_down, new_anchor, new_momentum


def solution(mesh):
    fine = Mesh(mesh.devices.reshape(4, 2, 2, 4, 8), ("yh", "core", "yl", "x", "z"))
    fsdp, replica = ("yh", "core"), ("yl", "x", "z")
    placed = (
        P(replica, fsdp, None),
        P(replica, fsdp, None),
        P(fsdp, None),
        P(fsdp, None),
        P(None, fsdp),
        P(replica, fsdp, None),
        P(fsdp, None),
        P(fsdp, None),
    )
    return jax.shard_map(
        on_device,
        mesh=fine,
        in_specs=placed,
        out_specs=(
            P(replica, fsdp, None),
            P(replica, fsdp, None),
            P(replica, None, fsdp),
            P(fsdp, None),
            P(fsdp, None),
        ),
        check_vma=False,
    )
```

```python
import functools

import jax
import jax.numpy as jnp
from jax import lax
from jax.experimental import pallas as pl
from jax.experimental.pallas import tpu as pltpu
from jax.sharding import Mesh
from jax.sharding import PartitionSpec as P

CHIPS = 4
ROWS = 128
WIDE = 1024
HALF = 512
HID = 256
DEAR = 100
VMEM_LIMIT = 63 * 1024 * 1024

F32 = jnp.float32
BF16 = jnp.bfloat16
ANY = pl.BlockSpec(memory_space=pl.ANY)
VMEM = pl.BlockSpec(memory_space=pltpu.VMEM)
SMEM = pl.BlockSpec(memory_space=pltpu.SMEM)


def run_copies(copies, sems):
    started = [pltpu.make_async_copy(src, dst, sems.at[i]) for i, (src, dst) in enumerate(copies)]
    for copy in started:
        copy.start()
    for copy in started:
        copy.wait()


def columns(base):
    return pl.ds(pl.multiple_of(base, HALF), HALF)


def wide_columns(chip):
    return pl.ds(pl.multiple_of(chip * WIDE, WIDE), WIDE)


def share_kernel(parts, place, gate, up, down, out, sems):
    gate_rows, down_rows = HALF // parts, HID // parts
    cut = 2 * gate_rows
    at_gate = pl.ds(pl.multiple_of(place[1] * gate_rows, gate_rows), gate_rows)
    at_down = pl.ds(pl.multiple_of(place[1] * down_rows, down_rows), down_rows)
    copies = [
        (gate.at[at_gate], out.at[pl.ds(0, gate_rows)]),
        (up.at[at_gate], out.at[pl.ds(gate_rows, gate_rows)]),
        (down.at[at_down, :HID], out.at[pl.ds(cut, down_rows)]),
        (down.at[at_down, HID:], out.at[pl.ds(cut + down_rows, down_rows)]),
    ]
    run_copies(copies, sems)


def own_share(place, gate, up, down, parts):
    return pl.pallas_call(
        functools.partial(share_kernel, parts),
        out_shape=jax.ShapeDtypeStruct((2 * (HALF + HID) // parts, HID), BF16),
        in_specs=[SMEM, ANY, ANY, ANY],
        out_specs=VMEM,
        scratch_shapes=[pltpu.SemaphoreType.DMA((4,))],
        compiler_params=pltpu.CompilerParams(vmem_limit_bytes=VMEM_LIMIT),
        cost_estimate=pl.CostEstimate(flops=0, bytes_accessed=1 << 18, transcendentals=0),
        name="weight_share",
    )(place, gate, up, down)


def beside_kernel(place, x, dy, after, out, sems):
    del after
    copies = []
    for i in range(CHIPS):
        other = columns(i * WIDE + (1 - place[0]) * HALF)
        copies += [(x.at[:, other], out.at[i, 0]), (dy.at[:, other], out.at[i, 1])]
    run_copies(copies, sems)


def for_beside(place, x, dy, after):
    return pl.pallas_call(
        beside_kernel,
        out_shape=jax.ShapeDtypeStruct((CHIPS, 2, ROWS, HALF), BF16),
        in_specs=[SMEM] + [ANY] * 3,
        out_specs=VMEM,
        scratch_shapes=[pltpu.SemaphoreType.DMA((8,))],
        compiler_params=pltpu.CompilerParams(vmem_limit_bytes=VMEM_LIMIT),
        cost_estimate=pl.CostEstimate(flops=0, bytes_accessed=2 << 20, transcendentals=0),
        name="tokens_beside",
    )(place, x, dy, after)


def pack_kernel(waited, place, x, dy, *rest):
    ahead, back, sems = rest[waited:]
    chip = place[2]
    near, far, last = (wide_columns(lax.rem(chip + shift, CHIPS)) for shift in (1, 2, 3))
    copies = [
        (x.at[:, near], ahead.at[0]),
        (dy.at[:, near], ahead.at[1]),
        (x.at[:, far], ahead.at[2]),
        (x.at[:, last], back.at[0]),
        (dy.at[:, last], back.at[1]),
        (dy.at[:, far], back.at[2]),
    ]
    run_copies(copies, sems)


def pack(place, x, dy, after):
    wide = jax.ShapeDtypeStruct((3, ROWS, WIDE), BF16)
    return pl.pallas_call(
        functools.partial(pack_kernel, len(after)),
        out_shape=(wide, wide),
        in_specs=[SMEM] + [ANY] * (2 + len(after)),
        out_specs=(VMEM, VMEM),
        scratch_shapes=[pltpu.SemaphoreType.DMA((6,))],
        compiler_params=pltpu.CompilerParams(vmem_limit_bytes=VMEM_LIMIT),
        cost_estimate=pl.CostEstimate(flops=0, bytes_accessed=4 << 20, transcendentals=0),
        name="pack_tokens",
    )(place, x, dy, *after)


def onward_kernel(ahead, back, far_x, far_dy, sems):
    run_copies([(ahead.at[2], far_x.at[0]), (back.at[2], far_dy.at[0])], sems)


def onward(ahead, back):
    one = jax.ShapeDtypeStruct((1, ROWS, WIDE), BF16)
    return pl.pallas_call(
        onward_kernel,
        out_shape=(one, one),
        in_specs=[ANY, ANY],
        out_specs=(VMEM, VMEM),
        scratch_shapes=[pltpu.SemaphoreType.DMA((2,))],
        compiler_params=pltpu.CompilerParams(vmem_limit_bytes=VMEM_LIMIT),
        cost_estimate=pl.CostEstimate(flops=0, bytes_accessed=DEAR << 20, transcendentals=0),
        name="onward",
    )(ahead, back)


def repack_kernel(place, ahead, back, far_x, far_dy, out, sems):
    other = columns((1 - place[0]) * HALF)
    copies = []
    for i, (a, b) in enumerate(((ahead.at[0], ahead.at[1]), (far_x.at[0], far_dy.at[0]), (back.at[0], back.at[1]))):
        copies += [(a.at[:, other], out.at[i, 0]), (b.at[:, other], out.at[i, 1])]
    run_copies(copies, sems)


def repack(place, arrived):
    return pl.pallas_call(
        repack_kernel,
        out_shape=jax.ShapeDtypeStruct((CHIPS - 1, 2, ROWS, HALF), BF16),
        in_specs=[SMEM] + [ANY] * 4,
        out_specs=VMEM,
        scratch_shapes=[pltpu.SemaphoreType.DMA((6,))],
        compiler_params=pltpu.CompilerParams(vmem_limit_bytes=VMEM_LIMIT),
        cost_estimate=pl.CostEstimate(flops=0, bytes_accessed=DEAR * 2 << 20, transcendentals=0),
        name="repack_tokens",
    )(place, *arrived)


def staged_kernel(delta, after, out, sem):
    del after
    run_copies([(delta, out)], sem)


def staged(delta, after):
    return pl.pallas_call(
        staged_kernel,
        out_shape=jax.ShapeDtypeStruct(delta.shape, delta.dtype),
        in_specs=[ANY, ANY],
        out_specs=VMEM,
        scratch_shapes=[pltpu.SemaphoreType.DMA((1,))],
        compiler_params=pltpu.CompilerParams(vmem_limit_bytes=VMEM_LIMIT),
        cost_estimate=pl.CostEstimate(flops=0, bytes_accessed=1 << 19, transcendentals=0),
        name="delta_staged",
    )(delta, after)


def hidden_kernel(parts, waited, place, x, dy, beside, *rest):
    weights = rest[:parts]
    mine, theirs, xs, dys, gates, ups, downs, sems = rest[parts + waited :]
    gate_rows, down_rows = HALF // parts, HID // parts
    cut = 2 * gate_rows
    copies = []
    for shift in range(CHIPS):
        chip = lax.rem(place[2] + shift, CHIPS)
        own = columns(chip * WIDE + place[0] * HALF)
        copies += [
            (x.at[:, own], xs.at[shift, :ROWS]),
            (dy.at[:, own], dys.at[shift, :ROWS]),
            (beside.at[chip, 0], xs.at[shift, ROWS:]),
            (beside.at[chip, 1], dys.at[shift, ROWS:]),
        ]
    for shift, ref in enumerate(weights):
        part = lax.rem(place[1] + shift, parts)
        to_gate = pl.ds(pl.multiple_of(part * gate_rows, gate_rows), gate_rows)
        to_down = pl.ds(pl.multiple_of(part * down_rows, down_rows), down_rows)
        copies += [
            (ref.at[:, pl.ds(0, gate_rows)], gates.at[:, to_gate]),
            (ref.at[:, pl.ds(gate_rows, gate_rows)], ups.at[:, to_gate]),
            (ref.at[:, pl.ds(cut, down_rows)], downs.at[:, 0, to_down]),
            (ref.at[:, pl.ds(cut + down_rows, down_rows)], downs.at[:, 1, to_down]),
        ]
    run_copies(copies, sems)
    gate = up = dh = 0.0
    for chip in range(CHIPS):
        a, b = xs[chip], dys[chip]
        gate += jnp.dot(a, gates[chip], preferred_element_type=F32)
        up += jnp.dot(a, ups[chip], preferred_element_type=F32)
        for h in range(2):
            dh += lax.dot_general(
                b[:, HID * h : HID * (h + 1)],
                downs[chip, h],
                (((1,), (1,)), ((), ())),
                preferred_element_type=F32,
            )
    for i, value in enumerate((gate, up, dh)):
        mine[i] = value[:ROWS]
        theirs[i] = value[ROWS:]


def hidden_sums(place, x, dy, beside, weights, after):
    out = jax.ShapeDtypeStruct((3, ROWS, HID), F32)
    return pl.pallas_call(
        functools.partial(hidden_kernel, len(weights), len(after)),
        out_shape=(out, out),
        in_specs=[SMEM] + [ANY] * (3 + len(weights) + len(after)),
        out_specs=(VMEM, VMEM),
        scratch_shapes=[
            pltpu.VMEM((CHIPS, 2 * ROWS, HALF), BF16),
            pltpu.VMEM((CHIPS, 2 * ROWS, HALF), BF16),
            pltpu.VMEM((CHIPS, HALF, HID), BF16),
            pltpu.VMEM((CHIPS, HALF, HID), BF16),
            pltpu.VMEM((CHIPS, 2, HID, HID), BF16),
            pltpu.SemaphoreType.DMA((4 * len(weights) + 16,)),
        ],
        compiler_params=pltpu.CompilerParams(vmem_limit_bytes=VMEM_LIMIT),
        cost_estimate=pl.CostEstimate(flops=6 * 256 * 2048 * 256, bytes_accessed=6 << 20, transcendentals=0),
        name="hidden_sums",
    )(place, x, dy, beside, *weights, *after)


def activation_kernel(waited, mine_ref, arrived_ref, *rest):
    out, mine, arrived, sems = rest[waited:]
    run_copies([(mine_ref, mine), (arrived_ref, arrived)], sems)
    gate = mine[0] + arrived[0]
    up = mine[1] + arrived[1]
    dh = mine[2] + arrived[2]
    sig = jax.nn.sigmoid(gate)
    active = gate * sig
    slope = sig * (1.0 + gate * (1.0 - sig))
    for i, value in enumerate((dh * up * slope, dh * active, active * up)):
        for chip in range(CHIPS):
            out[chip, i] = value.astype(BF16)


def activation(mine, arrived, after):
    return pl.pallas_call(
        functools.partial(activation_kernel, len(after)),
        out_shape=jax.ShapeDtypeStruct((CHIPS, 3, ROWS, HID), BF16),
        in_specs=[ANY] * (2 + len(after)),
        out_specs=VMEM,
        scratch_shapes=[
            pltpu.VMEM((3, ROWS, HID), F32),
            pltpu.VMEM((3, ROWS, HID), F32),
            pltpu.SemaphoreType.DMA((2,)),
        ],
        compiler_params=pltpu.CompilerParams(vmem_limit_bytes=VMEM_LIMIT),
        cost_estimate=pl.CostEstimate(flops=20 * ROWS * HID, bytes_accessed=1 << 20, transcendentals=ROWS * HID),
        name="activation",
    )(mine, arrived, *after)


def grads_kernel(place, x, dy, beside, ahead, back, far_x, far_dy, swapped, *rest):
    acts, (gg, gu, gd, xs, dys, hs, sems) = rest[:2], rest[2:]
    core, chip = place[0], place[2]
    half, own = columns(core * HALF), columns(chip * WIDE + core * HALF)
    here = [(x.at[:, own], dy.at[:, own])]
    here += [
        (a.at[:, half], b.at[:, half])
        for a, b in ((ahead.at[0], ahead.at[1]), (far_x.at[0], far_dy.at[0]), (back.at[0], back.at[1]))
    ]
    there = [(beside.at[chip, 0], beside.at[chip, 1])]
    there += [(swapped.at[i, 0], swapped.at[i, 1]) for i in range(CHIPS - 1)]
    copies = []
    for i, (a, b) in enumerate(here + there):
        rows = pl.ds(i * ROWS, ROWS)
        source = lax.rem(chip + 2 * CHIPS - i, CHIPS)
        copies += [(a, xs.at[rows]), (b, dys.at[rows]), (acts[i // CHIPS].at[source], hs.at[:, rows])]
    run_copies(copies, sems)
    tall = (((0,), (0,)), ((), ()))
    gg[0] = lax.dot_general(xs[...], hs[0], tall, preferred_element_type=F32).astype(BF16)
    gu[0] = lax.dot_general(xs[...], hs[1], tall, preferred_element_type=F32).astype(BF16)
    gd[0] = lax.dot_general(hs[2], dys[...], tall, preferred_element_type=F32).astype(BF16)


def grads(place, x, dy, beside, arrived, swapped, acts):
    tokens = 2 * CHIPS * ROWS
    return pl.pallas_call(
        grads_kernel,
        out_shape=(
            jax.ShapeDtypeStruct((1, HALF, HID), BF16),
            jax.ShapeDtypeStruct((1, HALF, HID), BF16),
            jax.ShapeDtypeStruct((1, HID, HALF), BF16),
        ),
        in_specs=[SMEM] + [ANY] * (8 + len(acts)),
        out_specs=(VMEM,) * 3,
        scratch_shapes=[
            pltpu.VMEM((tokens, HALF), BF16),
            pltpu.VMEM((tokens, HALF), BF16),
            pltpu.VMEM((3, tokens, HID), BF16),
            pltpu.SemaphoreType.DMA((24,)),
        ],
        compiler_params=pltpu.CompilerParams(vmem_limit_bytes=VMEM_LIMIT),
        cost_estimate=pl.CostEstimate(flops=6 * 1024 * 512 * 256, bytes_accessed=5 << 20, transcendentals=0),
        name="weight_grads",
    )(place, x, dy, beside, *arrived, swapped, *acts)


def to_shift(value, shift):
    return lax.ppermute(value, "yh", [(i, (i + shift) % CHIPS) for i in range(CHIPS)])


def from_shift(value, shift):
    return lax.ppermute(value, "yh", [(i, (i - shift) % CHIPS) for i in range(CHIPS)])


def from_x(value, shift, size):
    return lax.ppermute(value, "x", [(i, (i - shift) % size) for i in range(size)])


def other_core(value):
    return lax.ppermute(value, "core", [(0, 1), (1, 0)])


def share_of_sum(delta):
    everyone = ("yl", "x", "z")
    count = lax.axis_size(everyone)
    rows, cols = delta.shape
    tiles = delta.reshape(rows // 8, 8, cols // 128, 128).transpose(0, 2, 1, 3).reshape(count, 8, 128)
    return jnp.sum(lax.all_to_all(tiles, everyone, 0, 0, tiled=True), axis=0, keepdims=True)


def whole_mean(part, shape):
    everyone = ("yl", "x", "z")
    count = lax.axis_size(everyone)
    rows, cols = shape
    whole = lax.all_to_all(jnp.broadcast_to(part / count, (count, 8, 128)), everyone, 0, 0, tiled=True)
    return whole.reshape(rows // 8, cols // 128, 8, 128).transpose(0, 2, 1, 3).reshape(rows, cols)


def on_device(tokens, cotangent, w_gate, w_up, w_down, delta, anchor, momentum):
    x, dy = tokens[0], cotangent[0]
    place = jnp.stack([lax.axis_index(name) for name in ("core", "x", "yh")]).astype(jnp.int32)
    parts = lax.axis_size("x")

    share = own_share(place, w_gate, w_up, w_down, parts)
    shares = {shift: from_shift(share, shift) for shift in (1, 2, 3)}
    shares = jnp.stack([share] + [shares[shift] for shift in (1, 2, 3)])
    weights = [shares] + [from_x(shares, shift, parts) for shift in range(1, parts)]

    beside = other_core(for_beside(place, x, dy, share))
    part = share_of_sum(staged(delta[0], beside))
    ahead, back = pack(place, x, dy, (beside,))
    ahead, back = to_shift(ahead, 1), to_shift(back, 3)
    far_x, far_dy = onward(ahead, back)
    far_x, far_dy = to_shift(far_x, 1), to_shift(far_dy, 3)
    arrived = [ahead, back, far_x, far_dy]
    repacked = repack(place, arrived)
    swapped = other_core(repacked)

    pseudo = whole_mean(part, anchor.shape)
    new_momentum = 0.9 * momentum + pseudo
    new_anchor = anchor - 0.7 * (pseudo + 0.9 * new_momentum)

    mine, theirs = hidden_sums(place, x, dy, beside, weights, (far_x, far_dy))
    acts = activation(mine, other_core(theirs), (pseudo,))
    acts = lax.all_to_all(acts, "yh", 0, 0, tiled=True)
    acts = (acts, other_core(acts))
    grad_gate, grad_up, grad_down = grads(place, x, dy, beside, arrived, swapped, acts)
    return grad_gate, grad_up, grad_down, new_anchor, new_momentum


def solution(mesh):
    fine = Mesh(mesh.devices.reshape(4, 2, 2, 4, 8), ("yh", "core", "yl", "x", "z"))
    fsdp, replica = ("yh", "core"), ("yl", "x", "z")
    placed = (
        P(replica, fsdp, None),
        P(replica, fsdp, None),
        P(fsdp, None),
        P(fsdp, None),
        P(None, fsdp),
        P(replica, fsdp, None),
        P(fsdp, None),
        P(fsdp, None),
    )
    return jax.shard_map(
        on_device,
        mesh=fine,
        in_specs=placed,
        out_specs=(
            P(replica, fsdp, None),
            P(replica, fsdp, None),
            P(replica, None, fsdp),
            P(fsdp, None),
            P(fsdp, None),
        ),
        check_vma=False,
    )
```

```python
import functools

import jax
import jax.numpy as jnp
from jax import lax
from jax.experimental import pallas as pl
from jax.experimental.pallas import tpu as pltpu
from jax.sharding import Mesh
from jax.sharding import PartitionSpec as P

CHIPS = 4
ROWS = 128
WIDE = 1024
HALF = 512
HID = 256
DEAR = 100
VMEM_LIMIT = 63 * 1024 * 1024

F32 = jnp.float32
BF16 = jnp.bfloat16
ANY = pl.BlockSpec(memory_space=pl.ANY)
VMEM = pl.BlockSpec(memory_space=pltpu.VMEM)
SMEM = pl.BlockSpec(memory_space=pltpu.SMEM)


def run_copies(copies, sems):
    started = [pltpu.make_async_copy(src, dst, sems.at[i]) for i, (src, dst) in enumerate(copies)]
    for copy in started:
        copy.start()
    for copy in started:
        copy.wait()


def columns(base):
    return pl.ds(pl.multiple_of(base, HALF), HALF)


def wide_columns(chip):
    return pl.ds(pl.multiple_of(chip * WIDE, WIDE), WIDE)


def share_kernel(parts, place, gate, up, down, out, sems):
    gate_rows, down_rows = HALF // parts, HID // parts
    cut = 2 * gate_rows
    at_gate = pl.ds(pl.multiple_of(place[1] * gate_rows, gate_rows), gate_rows)
    at_down = pl.ds(pl.multiple_of(place[1] * down_rows, down_rows), down_rows)
    copies = [
        (gate.at[at_gate], out.at[pl.ds(0, gate_rows)]),
        (up.at[at_gate], out.at[pl.ds(gate_rows, gate_rows)]),
        (down.at[at_down, :HID], out.at[pl.ds(cut, down_rows)]),
        (down.at[at_down, HID:], out.at[pl.ds(cut + down_rows, down_rows)]),
    ]
    run_copies(copies, sems)


def own_share(place, gate, up, down, parts):
    return pl.pallas_call(
        functools.partial(share_kernel, parts),
        out_shape=jax.ShapeDtypeStruct((2 * (HALF + HID) // parts, HID), BF16),
        in_specs=[SMEM, ANY, ANY, ANY],
        out_specs=VMEM,
        scratch_shapes=[pltpu.SemaphoreType.DMA((4,))],
        compiler_params=pltpu.CompilerParams(vmem_limit_bytes=VMEM_LIMIT),
        cost_estimate=pl.CostEstimate(flops=0, bytes_accessed=1 << 18, transcendentals=0),
        name="weight_share",
    )(place, gate, up, down)


def beside_kernel(place, x, dy, after, out, sems):
    del after
    copies = []
    for i in range(CHIPS):
        other = columns(i * WIDE + (1 - place[0]) * HALF)
        copies += [(x.at[:, other], out.at[i, 0]), (dy.at[:, other], out.at[i, 1])]
    run_copies(copies, sems)


def for_beside(place, x, dy, after):
    return pl.pallas_call(
        beside_kernel,
        out_shape=jax.ShapeDtypeStruct((CHIPS, 2, ROWS, HALF), BF16),
        in_specs=[SMEM] + [ANY] * 3,
        out_specs=VMEM,
        scratch_shapes=[pltpu.SemaphoreType.DMA((8,))],
        compiler_params=pltpu.CompilerParams(vmem_limit_bytes=VMEM_LIMIT),
        cost_estimate=pl.CostEstimate(flops=0, bytes_accessed=2 << 20, transcendentals=0),
        name="tokens_beside",
    )(place, x, dy, after)


def pack_kernel(waited, place, x, dy, *rest):
    ahead, back, sems = rest[waited:]
    chip = place[2]
    near, far, last = (wide_columns(lax.rem(chip + shift, CHIPS)) for shift in (1, 2, 3))
    copies = [
        (x.at[:, near], ahead.at[0]),
        (dy.at[:, near], ahead.at[1]),
        (x.at[:, far], ahead.at[2]),
        (x.at[:, last], back.at[0]),
        (dy.at[:, last], back.at[1]),
        (dy.at[:, far], back.at[2]),
    ]
    run_copies(copies, sems)


def pack(place, x, dy, after):
    wide = jax.ShapeDtypeStruct((3, ROWS, WIDE), BF16)
    return pl.pallas_call(
        functools.partial(pack_kernel, len(after)),
        out_shape=(wide, wide),
        in_specs=[SMEM] + [ANY] * (2 + len(after)),
        out_specs=(VMEM, VMEM),
        scratch_shapes=[pltpu.SemaphoreType.DMA((6,))],
        compiler_params=pltpu.CompilerParams(vmem_limit_bytes=VMEM_LIMIT),
        cost_estimate=pl.CostEstimate(flops=0, bytes_accessed=4 << 20, transcendentals=0),
        name="pack_tokens",
    )(place, x, dy, *after)


def onward_kernel(ahead, back, far_x, far_dy, sems):
    run_copies([(ahead.at[2], far_x.at[0]), (back.at[2], far_dy.at[0])], sems)


def onward(ahead, back):
    one = jax.ShapeDtypeStruct((1, ROWS, WIDE), BF16)
    return pl.pallas_call(
        onward_kernel,
        out_shape=(one, one),
        in_specs=[ANY, ANY],
        out_specs=(VMEM, VMEM),
        scratch_shapes=[pltpu.SemaphoreType.DMA((2,))],
        compiler_params=pltpu.CompilerParams(vmem_limit_bytes=VMEM_LIMIT),
        cost_estimate=pl.CostEstimate(flops=0, bytes_accessed=DEAR << 20, transcendentals=0),
        name="onward",
    )(ahead, back)


def repack_kernel(place, ahead, back, far_x, far_dy, out, sems):
    other = columns((1 - place[0]) * HALF)
    copies = []
    for i, (a, b) in enumerate(((ahead.at[0], ahead.at[1]), (far_x.at[0], far_dy.at[0]), (back.at[0], back.at[1]))):
        copies += [(a.at[:, other], out.at[i, 0]), (b.at[:, other], out.at[i, 1])]
    run_copies(copies, sems)


def repack(place, arrived):
    return pl.pallas_call(
        repack_kernel,
        out_shape=jax.ShapeDtypeStruct((CHIPS - 1, 2, ROWS, HALF), BF16),
        in_specs=[SMEM] + [ANY] * 4,
        out_specs=VMEM,
        scratch_shapes=[pltpu.SemaphoreType.DMA((6,))],
        compiler_params=pltpu.CompilerParams(vmem_limit_bytes=VMEM_LIMIT),
        cost_estimate=pl.CostEstimate(flops=0, bytes_accessed=DEAR * 2 << 20, transcendentals=0),
        name="repack_tokens",
    )(place, *arrived)


def staged_kernel(delta, after, out, sem):
    del after
    run_copies([(delta, out)], sem)


def staged(delta, after):
    return pl.pallas_call(
        staged_kernel,
        out_shape=jax.ShapeDtypeStruct(delta.shape, delta.dtype),
        in_specs=[ANY, ANY],
        out_specs=VMEM,
        scratch_shapes=[pltpu.SemaphoreType.DMA((1,))],
        compiler_params=pltpu.CompilerParams(vmem_limit_bytes=VMEM_LIMIT),
        cost_estimate=pl.CostEstimate(flops=0, bytes_accessed=1 << 19, transcendentals=0),
        name="delta_staged",
    )(delta, after)


def hidden_kernel(parts, waited, place, x, dy, beside, *rest):
    weights = rest[:parts]
    mine, theirs, xs, dys, gates, ups, downs, sems = rest[parts + waited :]
    gate_rows, down_rows = HALF // parts, HID // parts
    cut = 2 * gate_rows
    copies = []
    for shift in range(CHIPS):
        chip = lax.rem(place[2] + shift, CHIPS)
        own = columns(chip * WIDE + place[0] * HALF)
        copies += [
            (x.at[:, own], xs.at[shift, :ROWS]),
            (dy.at[:, own], dys.at[shift, :ROWS]),
            (beside.at[chip, 0], xs.at[shift, ROWS:]),
            (beside.at[chip, 1], dys.at[shift, ROWS:]),
        ]
    for shift, ref in enumerate(weights):
        part = lax.rem(place[1] + shift, parts)
        to_gate = pl.ds(pl.multiple_of(part * gate_rows, gate_rows), gate_rows)
        to_down = pl.ds(pl.multiple_of(part * down_rows, down_rows), down_rows)
        copies += [
            (ref.at[:, pl.ds(0, gate_rows)], gates.at[:, to_gate]),
            (ref.at[:, pl.ds(gate_rows, gate_rows)], ups.at[:, to_gate]),
            (ref.at[:, pl.ds(cut, down_rows)], downs.at[:, 0, to_down]),
            (ref.at[:, pl.ds(cut + down_rows, down_rows)], downs.at[:, 1, to_down]),
        ]
    run_copies(copies, sems)
    gate = up = dh = 0.0
    for chip in range(CHIPS):
        a, b = xs[chip], dys[chip]
        gate += jnp.dot(a, gates[chip], preferred_element_type=F32)
        up += jnp.dot(a, ups[chip], preferred_element_type=F32)
        for h in range(2):
            dh += lax.dot_general(
                b[:, HID * h : HID * (h + 1)],
                downs[chip, h],
                (((1,), (1,)), ((), ())),
                preferred_element_type=F32,
            )
    for i, value in enumerate((gate, up, dh)):
        mine[i] = value[:ROWS]
        theirs[i] = value[ROWS:]


def hidden_sums(place, x, dy, beside, weights, after):
    out = jax.ShapeDtypeStruct((3, ROWS, HID), F32)
    return pl.pallas_call(
        functools.partial(hidden_kernel, len(weights), len(after)),
        out_shape=(out, out),
        in_specs=[SMEM] + [ANY] * (3 + len(weights) + len(after)),
        out_specs=(VMEM, VMEM),
        scratch_shapes=[
            pltpu.VMEM((CHIPS, 2 * ROWS, HALF), BF16),
            pltpu.VMEM((CHIPS, 2 * ROWS, HALF), BF16),
            pltpu.VMEM((CHIPS, HALF, HID), BF16),
            pltpu.VMEM((CHIPS, HALF, HID), BF16),
            pltpu.VMEM((CHIPS, 2, HID, HID), BF16),
            pltpu.SemaphoreType.DMA((4 * len(weights) + 16,)),
        ],
        compiler_params=pltpu.CompilerParams(vmem_limit_bytes=VMEM_LIMIT),
        cost_estimate=pl.CostEstimate(flops=6 * 256 * 2048 * 256, bytes_accessed=6 << 20, transcendentals=0),
        name="hidden_sums",
    )(place, x, dy, beside, *weights, *after)


def activation_kernel(waited, mine_ref, arrived_ref, *rest):
    out, mine, arrived, sems = rest[waited:]
    run_copies([(mine_ref, mine), (arrived_ref, arrived)], sems)
    gate = mine[0] + arrived[0]
    up = mine[1] + arrived[1]
    dh = mine[2] + arrived[2]
    sig = jax.nn.sigmoid(gate)
    active = gate * sig
    slope = sig * (1.0 + gate * (1.0 - sig))
    for i, value in enumerate((dh * up * slope, dh * active, active * up)):
        for chip in range(CHIPS):
            out[chip, i] = value.astype(BF16)


def activation(mine, arrived, after):
    return pl.pallas_call(
        functools.partial(activation_kernel, len(after)),
        out_shape=jax.ShapeDtypeStruct((CHIPS, 3, ROWS, HID), BF16),
        in_specs=[ANY] * (2 + len(after)),
        out_specs=VMEM,
        scratch_shapes=[
            pltpu.VMEM((3, ROWS, HID), F32),
            pltpu.VMEM((3, ROWS, HID), F32),
            pltpu.SemaphoreType.DMA((2,)),
        ],
        compiler_params=pltpu.CompilerParams(vmem_limit_bytes=VMEM_LIMIT),
        cost_estimate=pl.CostEstimate(flops=20 * ROWS * HID, bytes_accessed=1 << 20, transcendentals=ROWS * HID),
        name="activation",
    )(mine, arrived, *after)


def grads_kernel(place, x, dy, beside, ahead, back, far_x, far_dy, swapped, *rest):
    acts, (gg, gu, gd, xs, dys, hs, sems) = rest[:2], rest[2:]
    core, chip = place[0], place[2]
    half, own = columns(core * HALF), columns(chip * WIDE + core * HALF)
    here = [(x.at[:, own], dy.at[:, own])]
    here += [
        (a.at[:, half], b.at[:, half])
        for a, b in ((ahead.at[0], ahead.at[1]), (far_x.at[0], far_dy.at[0]), (back.at[0], back.at[1]))
    ]
    there = [(beside.at[chip, 0], beside.at[chip, 1])]
    there += [(swapped.at[i, 0], swapped.at[i, 1]) for i in range(CHIPS - 1)]
    copies = []
    for i, (a, b) in enumerate(here + there):
        rows = pl.ds(i * ROWS, ROWS)
        source = lax.rem(chip + 2 * CHIPS - i, CHIPS)
        copies += [(a, xs.at[rows]), (b, dys.at[rows]), (acts[i // CHIPS].at[source], hs.at[:, rows])]
    run_copies(copies, sems)
    tall = (((0,), (0,)), ((), ()))
    gg[0] = lax.dot_general(xs[...], hs[0], tall, preferred_element_type=F32).astype(BF16)
    gu[0] = lax.dot_general(xs[...], hs[1], tall, preferred_element_type=F32).astype(BF16)
    gd[0] = lax.dot_general(hs[2], dys[...], tall, preferred_element_type=F32).astype(BF16)


def grads(place, x, dy, beside, arrived, swapped, acts):
    tokens = 2 * CHIPS * ROWS
    return pl.pallas_call(
        grads_kernel,
        out_shape=(
            jax.ShapeDtypeStruct((1, HALF, HID), BF16),
            jax.ShapeDtypeStruct((1, HALF, HID), BF16),
            jax.ShapeDtypeStruct((1, HID, HALF), BF16),
        ),
        in_specs=[SMEM] + [ANY] * (8 + len(acts)),
        out_specs=(VMEM,) * 3,
        scratch_shapes=[
            pltpu.VMEM((tokens, HALF), BF16),
            pltpu.VMEM((tokens, HALF), BF16),
            pltpu.VMEM((3, tokens, HID), BF16),
            pltpu.SemaphoreType.DMA((24,)),
        ],
        compiler_params=pltpu.CompilerParams(vmem_limit_bytes=VMEM_LIMIT),
        cost_estimate=pl.CostEstimate(flops=6 * 1024 * 512 * 256, bytes_accessed=5 << 20, transcendentals=0),
        name="weight_grads",
    )(place, x, dy, beside, *arrived, swapped, *acts)


def to_shift(value, shift):
    return lax.ppermute(value, "yh", [(i, (i + shift) % CHIPS) for i in range(CHIPS)])


def from_shift(value, shift):
    return lax.ppermute(value, "yh", [(i, (i - shift) % CHIPS) for i in range(CHIPS)])


def from_x(value, shift, size):
    return lax.ppermute(value, "x", [(i, (i - shift) % size) for i in range(size)])


def other_core(value):
    return lax.ppermute(value, "core", [(0, 1), (1, 0)])


def mean_kernel(waited, parts, *rest):
    out, held, sems = rest[waited:]
    run_copies([(parts, held)], sems)
    count = parts.shape[0]
    mean = jnp.sum(held[...], axis=0, keepdims=True) / count
    out[...] = jnp.broadcast_to(mean, out.shape)


def mean_tile(parts, after):
    return pl.pallas_call(
        functools.partial(mean_kernel, len(after)),
        out_shape=jax.ShapeDtypeStruct(parts.shape, F32),
        in_specs=[ANY] * (1 + len(after)),
        out_specs=VMEM,
        scratch_shapes=[pltpu.VMEM(parts.shape, F32), pltpu.SemaphoreType.DMA((1,))],
        compiler_params=pltpu.CompilerParams(vmem_limit_bytes=VMEM_LIMIT),
        cost_estimate=pl.CostEstimate(flops=1 << 16, bytes_accessed=1 << 19, transcendentals=0),
        name="mean_tile",
    )(parts, *after)


def mean_of_replicas(delta, after):
    everyone = ("yl", "x", "z")
    count = lax.axis_size(everyone)
    rows, cols = delta.shape
    tiles = delta.reshape(rows // 8, 8, cols // 128, 128).transpose(0, 2, 1, 3).reshape(count, 8, 128)
    mean = mean_tile(lax.all_to_all(tiles, everyone, 0, 0, tiled=True), after)
    whole = lax.all_to_all(mean, everyone, 0, 0, tiled=True)
    return whole.reshape(rows // 8, cols // 128, 8, 128).transpose(0, 2, 1, 3).reshape(rows, cols)


def on_device(tokens, cotangent, w_gate, w_up, w_down, delta, anchor, momentum):
    x, dy = tokens[0], cotangent[0]
    place = jnp.stack([lax.axis_index(name) for name in ("core", "x", "yh")]).astype(jnp.int32)
    parts = lax.axis_size("x")

    share = own_share(place, w_gate, w_up, w_down, parts)
    shares = {shift: from_shift(share, shift) for shift in (1, 2, 3)}
    shares = jnp.stack([share] + [shares[shift] for shift in (1, 2, 3)])
    weights = [shares] + [from_x(shares, shift, parts) for shift in range(1, parts)]

    beside = other_core(for_beside(place, x, dy, share))
    held = staged(delta[0], beside)
    ahead, back = pack(place, x, dy, (shares, beside))
    ahead, back = to_shift(ahead, 1), to_shift(back, 3)
    handed_on = onward(ahead, back)
    far_x, far_dy = handed_on
    far_x, far_dy = to_shift(far_x, 1), to_shift(far_dy, 3)
    arrived = [ahead, back, far_x, far_dy]
    repacked = repack(place, arrived)
    swapped = other_core(repacked)

    pseudo = mean_of_replicas(held, handed_on)
    new_momentum = 0.9 * momentum + pseudo
    new_anchor = anchor - 0.7 * (pseudo + 0.9 * new_momentum)

    mine, theirs = hidden_sums(place, x, dy, beside, weights, (far_x, far_dy))
    acts = activation(mine, other_core(theirs), (pseudo,))
    acts = lax.all_to_all(acts, "yh", 0, 0, tiled=True)
    acts = (acts, other_core(acts))
    grad_gate, grad_up, grad_down = grads(place, x, dy, beside, arrived, swapped, acts)
    return grad_gate, grad_up, grad_down, new_anchor, new_momentum


def solution(mesh):
    fine = Mesh(mesh.devices.reshape(4, 2, 2, 4, 8), ("yh", "core", "yl", "x", "z"))
    fsdp, replica = ("yh", "core"), ("yl", "x", "z")
    placed = (
        P(replica, fsdp, None),
        P(replica, fsdp, None),
        P(fsdp, None),
        P(fsdp, None),
        P(None, fsdp),
        P(replica, fsdp, None),
        P(fsdp, None),
        P(fsdp, None),
    )
    return jax.shard_map(
        on_device,
        mesh=fine,
        in_specs=placed,
        out_specs=(
            P(replica, fsdp, None),
            P(replica, fsdp, None),
            P(replica, None, fsdp),
            P(fsdp, None),
            P(fsdp, None),
        ),
        check_vma=False,
    )
```

```python
import functools

import jax
import jax.numpy as jnp
from jax import lax
from jax.experimental import pallas as pl
from jax.experimental.pallas import tpu as pltpu
from jax.sharding import Mesh
from jax.sharding import PartitionSpec as P

CHIPS = 4
ROWS = 128
WIDE = 1024
HALF = 512
HID = 256
DEAR = 100
VMEM_LIMIT = 63 * 1024 * 1024

F32 = jnp.float32
BF16 = jnp.bfloat16
ANY = pl.BlockSpec(memory_space=pl.ANY)
VMEM = pl.BlockSpec(memory_space=pltpu.VMEM)
SMEM = pl.BlockSpec(memory_space=pltpu.SMEM)


def start_copies(copies, sems):
    started = [pltpu.make_async_copy(src, dst, sems.at[i]) for i, (src, dst) in enumerate(copies)]
    for copy in started:
        copy.start()
    return started


def wait_copies(started):
    for copy in started:
        copy.wait()


def run_copies(copies, sems):
    wait_copies(start_copies(copies, sems))


def columns(base):
    return pl.ds(pl.multiple_of(base, HALF), HALF)


def wide_columns(chip):
    return pl.ds(pl.multiple_of(chip * WIDE, WIDE), WIDE)


def share_kernel(parts, place, gate, up, down, out, sems):
    gate_rows, down_rows = HALF // parts, HID // parts
    cut = 2 * gate_rows
    at_gate = pl.ds(pl.multiple_of(place[1] * gate_rows, gate_rows), gate_rows)
    at_down = pl.ds(pl.multiple_of(place[1] * down_rows, down_rows), down_rows)
    copies = [
        (gate.at[at_gate], out.at[pl.ds(0, gate_rows)]),
        (up.at[at_gate], out.at[pl.ds(gate_rows, gate_rows)]),
        (down.at[at_down, :HID], out.at[pl.ds(cut, down_rows)]),
        (down.at[at_down, HID:], out.at[pl.ds(cut + down_rows, down_rows)]),
    ]
    run_copies(copies, sems)


def own_share(place, gate, up, down, parts):
    return pl.pallas_call(
        functools.partial(share_kernel, parts),
        out_shape=jax.ShapeDtypeStruct((2 * (HALF + HID) // parts, HID), BF16),
        in_specs=[SMEM, ANY, ANY, ANY],
        out_specs=VMEM,
        scratch_shapes=[pltpu.SemaphoreType.DMA((4,))],
        compiler_params=pltpu.CompilerParams(vmem_limit_bytes=VMEM_LIMIT),
        cost_estimate=pl.CostEstimate(flops=0, bytes_accessed=1 << 18, transcendentals=0),
        name="weight_share",
    )(place, gate, up, down)


def beside_kernel(place, x, dy, after, out, sems):
    del after
    copies = []
    for i in range(CHIPS):
        other = columns(i * WIDE + (1 - place[0]) * HALF)
        copies += [(x.at[:, other], out.at[i, 0]), (dy.at[:, other], out.at[i, 1])]
    run_copies(copies, sems)


def for_beside(place, x, dy, after):
    return pl.pallas_call(
        beside_kernel,
        out_shape=jax.ShapeDtypeStruct((CHIPS, 2, ROWS, HALF), BF16),
        in_specs=[SMEM] + [ANY] * 3,
        out_specs=VMEM,
        scratch_shapes=[pltpu.SemaphoreType.DMA((8,))],
        compiler_params=pltpu.CompilerParams(vmem_limit_bytes=VMEM_LIMIT),
        cost_estimate=pl.CostEstimate(flops=0, bytes_accessed=2 << 20, transcendentals=0),
        name="tokens_beside",
    )(place, x, dy, after)


def pack_kernel(waited, place, x, dy, *rest):
    ahead, back, sems = rest[waited:]
    chip = place[2]
    near, far, last = (wide_columns(lax.rem(chip + shift, CHIPS)) for shift in (1, 2, 3))
    copies = [
        (x.at[:, near], ahead.at[0]),
        (dy.at[:, near], ahead.at[1]),
        (x.at[:, far], ahead.at[2]),
        (x.at[:, last], back.at[0]),
        (dy.at[:, last], back.at[1]),
        (dy.at[:, far], back.at[2]),
    ]
    run_copies(copies, sems)


def pack(place, x, dy, after):
    wide = jax.ShapeDtypeStruct((3, ROWS, WIDE), BF16)
    return pl.pallas_call(
        functools.partial(pack_kernel, len(after)),
        out_shape=(wide, wide),
        in_specs=[SMEM] + [ANY] * (2 + len(after)),
        out_specs=(VMEM, VMEM),
        scratch_shapes=[pltpu.SemaphoreType.DMA((6,))],
        compiler_params=pltpu.CompilerParams(vmem_limit_bytes=VMEM_LIMIT),
        cost_estimate=pl.CostEstimate(flops=0, bytes_accessed=4 << 20, transcendentals=0),
        name="pack_tokens",
    )(place, x, dy, *after)


def onward_kernel(ahead, back, far_x, far_dy, sems):
    run_copies([(ahead.at[2], far_x.at[0]), (back.at[2], far_dy.at[0])], sems)


def onward(ahead, back):
    one = jax.ShapeDtypeStruct((1, ROWS, WIDE), BF16)
    return pl.pallas_call(
        onward_kernel,
        out_shape=(one, one),
        in_specs=[ANY, ANY],
        out_specs=(VMEM, VMEM),
        scratch_shapes=[pltpu.SemaphoreType.DMA((2,))],
        compiler_params=pltpu.CompilerParams(vmem_limit_bytes=VMEM_LIMIT),
        cost_estimate=pl.CostEstimate(flops=0, bytes_accessed=DEAR << 20, transcendentals=0),
        name="onward",
    )(ahead, back)


def repack_kernel(place, ahead, back, far_x, far_dy, out, sems):
    other = columns((1 - place[0]) * HALF)
    copies = []
    for i, (a, b) in enumerate(((ahead.at[0], ahead.at[1]), (far_x.at[0], far_dy.at[0]), (back.at[0], back.at[1]))):
        copies += [(a.at[:, other], out.at[i, 0]), (b.at[:, other], out.at[i, 1])]
    run_copies(copies, sems)


def repack(place, arrived):
    return pl.pallas_call(
        repack_kernel,
        out_shape=jax.ShapeDtypeStruct((CHIPS - 1, 2, ROWS, HALF), BF16),
        in_specs=[SMEM] + [ANY] * 4,
        out_specs=VMEM,
        scratch_shapes=[pltpu.SemaphoreType.DMA((6,))],
        compiler_params=pltpu.CompilerParams(vmem_limit_bytes=VMEM_LIMIT),
        cost_estimate=pl.CostEstimate(flops=0, bytes_accessed=DEAR * 2 << 20, transcendentals=0),
        name="repack_tokens",
    )(place, *arrived)


def staged_kernel(delta, after, out, sem):
    del after
    run_copies([(delta, out)], sem)


def staged(delta, after):
    return pl.pallas_call(
        staged_kernel,
        out_shape=jax.ShapeDtypeStruct(delta.shape, delta.dtype),
        in_specs=[ANY, ANY],
        out_specs=VMEM,
        scratch_shapes=[pltpu.SemaphoreType.DMA((1,))],
        compiler_params=pltpu.CompilerParams(vmem_limit_bytes=VMEM_LIMIT),
        cost_estimate=pl.CostEstimate(flops=0, bytes_accessed=1 << 19, transcendentals=0),
        name="delta_staged",
    )(delta, after)


def hidden_kernel(parts, waited, place, x, dy, beside, *rest):
    weights = rest[:parts]
    mine, theirs, xs, dys, gates, ups, downs, sems = rest[parts + waited :]
    gate_rows, down_rows = HALF // parts, HID // parts
    cut = 2 * gate_rows
    to_gate, to_up, to_down = [], [], []
    for shift in range(CHIPS):
        chip = lax.rem(place[2] + shift, CHIPS)
        own = columns(chip * WIDE + place[0] * HALF)
        to_gate += [(x.at[:, own], xs.at[shift, :ROWS]), (beside.at[chip, 0], xs.at[shift, ROWS:])]
        to_down += [(dy.at[:, own], dys.at[shift, :ROWS]), (beside.at[chip, 1], dys.at[shift, ROWS:])]
    for shift, ref in enumerate(weights):
        part = lax.rem(place[1] + shift, parts)
        gate_at = pl.ds(pl.multiple_of(part * gate_rows, gate_rows), gate_rows)
        down_at = pl.ds(pl.multiple_of(part * down_rows, down_rows), down_rows)
        to_gate.append((ref.at[:, pl.ds(0, gate_rows)], gates.at[:, gate_at]))
        to_up.append((ref.at[:, pl.ds(gate_rows, gate_rows)], ups.at[:, gate_at]))
        to_down += [
            (ref.at[:, pl.ds(cut, down_rows)], downs.at[:, 0, down_at]),
            (ref.at[:, pl.ds(cut + down_rows, down_rows)], downs.at[:, 1, down_at]),
        ]
    started = start_copies(to_gate + to_up + to_down, sems)
    first, second = len(to_gate), len(to_gate) + len(to_up)

    def put(i, value):
        mine[i] = value[:ROWS]
        theirs[i] = value[ROWS:]

    wait_copies(started[:first])
    put(0, sum(jnp.dot(xs[i], gates[i], preferred_element_type=F32) for i in range(CHIPS)))
    wait_copies(started[first:second])
    put(1, sum(jnp.dot(xs[i], ups[i], preferred_element_type=F32) for i in range(CHIPS)))
    wait_copies(started[second:])
    wide = (((1,), (1,)), ((), ()))
    put(
        2,
        sum(
            lax.dot_general(dys[i, :, HID * h : HID * (h + 1)], downs[i, h], wide, preferred_element_type=F32)
            for i in range(CHIPS)
            for h in range(2)
        ),
    )


def hidden_sums(place, x, dy, beside, weights, after):
    out = jax.ShapeDtypeStruct((3, ROWS, HID), F32)
    return pl.pallas_call(
        functools.partial(hidden_kernel, len(weights), len(after)),
        out_shape=(out, out),
        in_specs=[SMEM] + [ANY] * (3 + len(weights) + len(after)),
        out_specs=(VMEM, VMEM),
        scratch_shapes=[
            pltpu.VMEM((CHIPS, 2 * ROWS, HALF), BF16),
            pltpu.VMEM((CHIPS, 2 * ROWS, HALF), BF16),
            pltpu.VMEM((CHIPS, HALF, HID), BF16),
            pltpu.VMEM((CHIPS, HALF, HID), BF16),
            pltpu.VMEM((CHIPS, 2, HID, HID), BF16),
            pltpu.SemaphoreType.DMA((4 * len(weights) + 16,)),
        ],
        compiler_params=pltpu.CompilerParams(vmem_limit_bytes=VMEM_LIMIT),
        cost_estimate=pl.CostEstimate(flops=6 * 256 * 2048 * 256, bytes_accessed=6 << 20, transcendentals=0),
        name="hidden_sums",
    )(place, x, dy, beside, *weights, *after)


def activation_kernel(mine_ref, arrived_ref, after, out, mine, arrived, sems):
    del after
    run_copies([(mine_ref, mine), (arrived_ref, arrived)], sems)
    gate = mine[0] + arrived[0]
    up = mine[1] + arrived[1]
    dh = mine[2] + arrived[2]
    sig = jax.nn.sigmoid(gate)
    active = gate * sig
    slope = sig * (1.0 + gate * (1.0 - sig))
    for i, value in enumerate((dh * up * slope, dh * active, active * up)):
        for chip in range(CHIPS):
            out[chip, i] = value.astype(BF16)


def activation(mine, arrived, after):
    return pl.pallas_call(
        activation_kernel,
        out_shape=jax.ShapeDtypeStruct((CHIPS, 3, ROWS, HID), BF16),
        in_specs=[ANY] * 3,
        out_specs=VMEM,
        scratch_shapes=[
            pltpu.VMEM((3, ROWS, HID), F32),
            pltpu.VMEM((3, ROWS, HID), F32),
            pltpu.SemaphoreType.DMA((2,)),
        ],
        compiler_params=pltpu.CompilerParams(vmem_limit_bytes=VMEM_LIMIT),
        cost_estimate=pl.CostEstimate(flops=20 * ROWS * HID, bytes_accessed=1 << 20, transcendentals=ROWS * HID),
        name="activation",
    )(mine, arrived, after)


def grads_kernel(place, x, dy, beside, ahead, back, far_x, far_dy, swapped, *rest):
    acts, (gg, gu, gd, xs, dys, hs, sems) = rest[:2], rest[2:]
    core, chip = place[0], place[2]
    half, own = columns(core * HALF), columns(chip * WIDE + core * HALF)
    here = [(x.at[:, own], dy.at[:, own])]
    here += [
        (a.at[:, half], b.at[:, half])
        for a, b in ((ahead.at[0], ahead.at[1]), (far_x.at[0], far_dy.at[0]), (back.at[0], back.at[1]))
    ]
    there = [(beside.at[chip, 0], beside.at[chip, 1])]
    there += [(swapped.at[i, 0], swapped.at[i, 1]) for i in range(CHIPS - 1)]
    early, late = [], []
    for i, (a, b) in enumerate(here + there):
        rows = pl.ds(i * ROWS, ROWS)
        source = lax.rem(chip + 2 * CHIPS - i, CHIPS)
        early += [(acts[i // CHIPS].at[source], hs.at[:, rows]), (a, xs.at[rows])]
        late.append((b, dys.at[rows]))
    started = start_copies(early + late, sems)
    tall = (((0,), (0,)), ((), ()))
    wait_copies(started[: len(early)])
    gg[0] = lax.dot_general(xs[...], hs[0], tall, preferred_element_type=F32).astype(BF16)
    gu[0] = lax.dot_general(xs[...], hs[1], tall, preferred_element_type=F32).astype(BF16)
    wait_copies(started[len(early) :])
    gd[0] = lax.dot_general(hs[2], dys[...], tall, preferred_element_type=F32).astype(BF16)


def grads(place, x, dy, beside, arrived, swapped, acts):
    tokens = 2 * CHIPS * ROWS
    return pl.pallas_call(
        grads_kernel,
        out_shape=(
            jax.ShapeDtypeStruct((1, HALF, HID), BF16),
            jax.ShapeDtypeStruct((1, HALF, HID), BF16),
            jax.ShapeDtypeStruct((1, HID, HALF), BF16),
        ),
        in_specs=[SMEM] + [ANY] * (8 + len(acts)),
        out_specs=(VMEM,) * 3,
        scratch_shapes=[
            pltpu.VMEM((tokens, HALF), BF16),
            pltpu.VMEM((tokens, HALF), BF16),
            pltpu.VMEM((3, tokens, HID), BF16),
            pltpu.SemaphoreType.DMA((24,)),
        ],
        compiler_params=pltpu.CompilerParams(vmem_limit_bytes=VMEM_LIMIT),
        cost_estimate=pl.CostEstimate(flops=6 * 1024 * 512 * 256, bytes_accessed=5 << 20, transcendentals=0),
        name="weight_grads",
    )(place, x, dy, beside, *arrived, swapped, *acts)


def to_shift(value, shift):
    return lax.ppermute(value, "yh", [(i, (i + shift) % CHIPS) for i in range(CHIPS)])


def from_shift(value, shift):
    return lax.ppermute(value, "yh", [(i, (i - shift) % CHIPS) for i in range(CHIPS)])


def from_x(value, shift, size):
    return lax.ppermute(value, "x", [(i, (i - shift) % size) for i in range(size)])


def other_core(value):
    return lax.ppermute(value, "core", [(0, 1), (1, 0)])


def share_of_sum(delta):
    everyone = ("yl", "x", "z")
    count = lax.axis_size(everyone)
    rows, cols = delta.shape
    tiles = delta.reshape(rows // 8, 8, cols // 128, 128).transpose(0, 2, 1, 3).reshape(count, 8, 128)
    return jnp.sum(lax.all_to_all(tiles, everyone, 0, 0, tiled=True), axis=0, keepdims=True)


def whole_mean(part, shape):
    everyone = ("yl", "x", "z")
    count = lax.axis_size(everyone)
    rows, cols = shape
    whole = lax.all_to_all(jnp.broadcast_to(part / count, (count, 8, 128)), everyone, 0, 0, tiled=True)
    return whole.reshape(rows // 8, cols // 128, 8, 128).transpose(0, 2, 1, 3).reshape(rows, cols)


def on_device(tokens, cotangent, w_gate, w_up, w_down, delta, anchor, momentum):
    x, dy = tokens[0], cotangent[0]
    place = jnp.stack([lax.axis_index(name) for name in ("core", "x", "yh")]).astype(jnp.int32)
    parts = lax.axis_size("x")

    share = own_share(place, w_gate, w_up, w_down, parts)
    shares = {shift: from_shift(share, shift) for shift in (1, 2, 3)}
    shares = jnp.stack([share] + [shares[shift] for shift in (1, 2, 3)])
    weights = [shares] + [from_x(shares, shift, parts) for shift in range(1, parts)]

    beside = other_core(for_beside(place, x, dy, share))
    part = share_of_sum(staged(delta[0], beside))
    ahead, back = pack(place, x, dy, (shares, beside))
    ahead, back = to_shift(ahead, 1), to_shift(back, 3)
    far_x, far_dy = onward(ahead, back)
    far_x, far_dy = to_shift(far_x, 1), to_shift(far_dy, 3)
    arrived = [ahead, back, far_x, far_dy]
    repacked = repack(place, arrived)
    swapped = other_core(repacked)

    pseudo = whole_mean(part, anchor.shape)
    new_momentum = 0.9 * momentum + pseudo
    new_anchor = anchor - 0.7 * (pseudo + 0.9 * new_momentum)

    mine, theirs = hidden_sums(place, x, dy, beside, weights, (far_x, far_dy))
    acts = activation(mine, other_core(theirs), new_anchor)
    acts = lax.all_to_all(acts, "yh", 0, 0, tiled=True)
    acts = (acts, other_core(acts))
    grad_gate, grad_up, grad_down = grads(place, x, dy, beside, arrived, swapped, acts)
    return grad_gate, grad_up, grad_down, new_anchor, new_momentum


def solution(mesh):
    fine = Mesh(mesh.devices.reshape(4, 2, 2, 4, 8), ("yh", "core", "yl", "x", "z"))
    fsdp, replica = ("yh", "core"), ("yl", "x", "z")
    placed = (
        P(replica, fsdp, None),
        P(replica, fsdp, None),
        P(fsdp, None),
        P(fsdp, None),
        P(None, fsdp),
        P(replica, fsdp, None),
        P(fsdp, None),
        P(fsdp, None),
    )
    return jax.shard_map(
        on_device,
        mesh=fine,
        in_specs=placed,
        out_specs=(
            P(replica, fsdp, None),
            P(replica, fsdp, None),
            P(replica, None, fsdp),
            P(fsdp, None),
            P(fsdp, None),
        ),
        check_vma=False,
    )
```

```python
import functools

import jax
import jax.numpy as jnp
from jax import lax
from jax.experimental import pallas as pl
from jax.experimental.pallas import tpu as pltpu
from jax.sharding import Mesh
from jax.sharding import PartitionSpec as P

CHIPS = 4
ROWS = 128
WIDE = 1024
HALF = 512
HID = 256
DEAR = 100
VMEM_LIMIT = 63 * 1024 * 1024

F32 = jnp.float32
BF16 = jnp.bfloat16
ANY = pl.BlockSpec(memory_space=pl.ANY)
VMEM = pl.BlockSpec(memory_space=pltpu.VMEM)
SMEM = pl.BlockSpec(memory_space=pltpu.SMEM)


def start_copies(copies, sems):
    started = [pltpu.make_async_copy(src, dst, sems.at[i]) for i, (src, dst) in enumerate(copies)]
    for copy in started:
        copy.start()
    return started


def wait_copies(started):
    for copy in started:
        copy.wait()


def run_copies(copies, sems):
    wait_copies(start_copies(copies, sems))


def columns(base):
    return pl.ds(pl.multiple_of(base, HALF), HALF)


def wide_columns(chip):
    return pl.ds(pl.multiple_of(chip * WIDE, WIDE), WIDE)


def share_kernel(parts, place, gate, up, down, out, sems):
    gate_rows, down_rows = HALF // parts, HID // parts
    cut = 2 * gate_rows
    at_gate = pl.ds(pl.multiple_of(place[1] * gate_rows, gate_rows), gate_rows)
    at_down = pl.ds(pl.multiple_of(place[1] * down_rows, down_rows), down_rows)
    copies = [
        (gate.at[at_gate], out.at[pl.ds(0, gate_rows)]),
        (up.at[at_gate], out.at[pl.ds(gate_rows, gate_rows)]),
        (down.at[at_down, :HID], out.at[pl.ds(cut, down_rows)]),
        (down.at[at_down, HID:], out.at[pl.ds(cut + down_rows, down_rows)]),
    ]
    run_copies(copies, sems)


def own_share(place, gate, up, down, parts):
    return pl.pallas_call(
        functools.partial(share_kernel, parts),
        out_shape=jax.ShapeDtypeStruct((2 * (HALF + HID) // parts, HID), BF16),
        in_specs=[SMEM, ANY, ANY, ANY],
        out_specs=VMEM,
        scratch_shapes=[pltpu.SemaphoreType.DMA((4,))],
        compiler_params=pltpu.CompilerParams(vmem_limit_bytes=VMEM_LIMIT),
        cost_estimate=pl.CostEstimate(flops=0, bytes_accessed=1 << 18, transcendentals=0),
        name="weight_share",
    )(place, gate, up, down)


def pack_kernel(waited, place, x, dy, *rest):
    ahead, back, sems = rest[waited:]
    chip = place[2]
    near, far, last = (wide_columns(lax.rem(chip + shift, CHIPS)) for shift in (1, 2, 3))
    copies = [
        (x.at[:, near], ahead.at[0]),
        (dy.at[:, near], ahead.at[1]),
        (x.at[:, far], ahead.at[2]),
        (x.at[:, last], back.at[0]),
        (dy.at[:, last], back.at[1]),
        (dy.at[:, far], back.at[2]),
    ]
    run_copies(copies, sems)


def pack(place, x, dy, after):
    wide = jax.ShapeDtypeStruct((3, ROWS, WIDE), BF16)
    return pl.pallas_call(
        functools.partial(pack_kernel, len(after)),
        out_shape=(wide, wide),
        in_specs=[SMEM] + [ANY] * (2 + len(after)),
        out_specs=(VMEM, VMEM),
        scratch_shapes=[pltpu.SemaphoreType.DMA((6,))],
        compiler_params=pltpu.CompilerParams(vmem_limit_bytes=VMEM_LIMIT),
        cost_estimate=pl.CostEstimate(flops=0, bytes_accessed=4 << 20, transcendentals=0),
        name="pack_tokens",
    )(place, x, dy, *after)


def onward_kernel(ahead, back, far_x, far_dy, sems):
    run_copies([(ahead.at[2], far_x.at[0]), (back.at[2], far_dy.at[0])], sems)


def onward(ahead, back):
    one = jax.ShapeDtypeStruct((1, ROWS, WIDE), BF16)
    return pl.pallas_call(
        onward_kernel,
        out_shape=(one, one),
        in_specs=[ANY, ANY],
        out_specs=(VMEM, VMEM),
        scratch_shapes=[pltpu.SemaphoreType.DMA((2,))],
        compiler_params=pltpu.CompilerParams(vmem_limit_bytes=VMEM_LIMIT),
        cost_estimate=pl.CostEstimate(flops=0, bytes_accessed=DEAR << 20, transcendentals=0),
        name="onward",
    )(ahead, back)


def repack_kernel(place, ahead, back, far_x, far_dy, out, sems):
    other = columns((1 - place[0]) * HALF)
    copies = []
    for i, (a, b) in enumerate(((ahead.at[0], ahead.at[1]), (far_x.at[0], far_dy.at[0]), (back.at[0], back.at[1]))):
        copies += [(a.at[:, other], out.at[i, 0]), (b.at[:, other], out.at[i, 1])]
    run_copies(copies, sems)


def repack(place, arrived):
    return pl.pallas_call(
        repack_kernel,
        out_shape=jax.ShapeDtypeStruct((CHIPS - 1, 2, ROWS, HALF), BF16),
        in_specs=[SMEM] + [ANY] * 4,
        out_specs=VMEM,
        scratch_shapes=[pltpu.SemaphoreType.DMA((6,))],
        compiler_params=pltpu.CompilerParams(vmem_limit_bytes=VMEM_LIMIT),
        cost_estimate=pl.CostEstimate(flops=0, bytes_accessed=DEAR * 2 << 20, transcendentals=0),
        name="repack_tokens",
    )(place, *arrived)


def staged_kernel(delta, after, out, sem):
    del after
    run_copies([(delta, out)], sem)


def staged(delta, after):
    return pl.pallas_call(
        staged_kernel,
        out_shape=jax.ShapeDtypeStruct(delta.shape, delta.dtype),
        in_specs=[ANY, ANY],
        out_specs=VMEM,
        scratch_shapes=[pltpu.SemaphoreType.DMA((1,))],
        compiler_params=pltpu.CompilerParams(vmem_limit_bytes=VMEM_LIMIT),
        cost_estimate=pl.CostEstimate(flops=0, bytes_accessed=1 << 19, transcendentals=0),
        name="delta_staged",
    )(delta, after)


def hidden_kernel(parts, waited, place, x, dy, beside_x, beside_dy, *rest):
    weights = rest[:parts]
    mine, theirs, xs, dys, gates, ups, downs, sems = rest[parts + waited :]
    gate_rows, down_rows = HALF // parts, HID // parts
    cut = 2 * gate_rows
    to_gate, to_up, to_down = [], [], []
    for shift in range(CHIPS):
        chip = lax.rem(place[2] + shift, CHIPS)
        own = columns(chip * WIDE + place[0] * HALF)
        to_gate += [(x.at[:, own], xs.at[shift, :ROWS]), (beside_x.at[:, own], xs.at[shift, ROWS:])]
        to_down += [(dy.at[:, own], dys.at[shift, :ROWS]), (beside_dy.at[:, own], dys.at[shift, ROWS:])]
    for shift, ref in enumerate(weights):
        part = lax.rem(place[1] + shift, parts)
        gate_at = pl.ds(pl.multiple_of(part * gate_rows, gate_rows), gate_rows)
        down_at = pl.ds(pl.multiple_of(part * down_rows, down_rows), down_rows)
        to_gate.append((ref.at[:, pl.ds(0, gate_rows)], gates.at[:, gate_at]))
        to_up.append((ref.at[:, pl.ds(gate_rows, gate_rows)], ups.at[:, gate_at]))
        to_down += [
            (ref.at[:, pl.ds(cut, down_rows)], downs.at[:, 0, down_at]),
            (ref.at[:, pl.ds(cut + down_rows, down_rows)], downs.at[:, 1, down_at]),
        ]
    started = start_copies(to_gate + to_up + to_down, sems)
    first, second = len(to_gate), len(to_gate) + len(to_up)

    def put(i, value):
        mine[i] = value[:ROWS]
        theirs[i] = value[ROWS:]

    wait_copies(started[:first])
    put(0, sum(jnp.dot(xs[i], gates[i], preferred_element_type=F32) for i in range(CHIPS)))
    wait_copies(started[first:second])
    put(1, sum(jnp.dot(xs[i], ups[i], preferred_element_type=F32) for i in range(CHIPS)))
    wait_copies(started[second:])
    wide = (((1,), (1,)), ((), ()))
    put(
        2,
        sum(
            lax.dot_general(dys[i, :, HID * h : HID * (h + 1)], downs[i, h], wide, preferred_element_type=F32)
            for i in range(CHIPS)
            for h in range(2)
        ),
    )


def hidden_sums(place, x, dy, beside, weights, after):
    out = jax.ShapeDtypeStruct((3, ROWS, HID), F32)
    return pl.pallas_call(
        functools.partial(hidden_kernel, len(weights), len(after)),
        out_shape=(out, out),
        in_specs=[SMEM] + [ANY] * (4 + len(weights) + len(after)),
        out_specs=(VMEM, VMEM),
        scratch_shapes=[
            pltpu.VMEM((CHIPS, 2 * ROWS, HALF), BF16),
            pltpu.VMEM((CHIPS, 2 * ROWS, HALF), BF16),
            pltpu.VMEM((CHIPS, HALF, HID), BF16),
            pltpu.VMEM((CHIPS, HALF, HID), BF16),
            pltpu.VMEM((CHIPS, 2, HID, HID), BF16),
            pltpu.SemaphoreType.DMA((4 * len(weights) + 16,)),
        ],
        compiler_params=pltpu.CompilerParams(vmem_limit_bytes=VMEM_LIMIT),
        cost_estimate=pl.CostEstimate(flops=6 * 256 * 2048 * 256, bytes_accessed=6 << 20, transcendentals=0),
        name="hidden_sums",
    )(place, x, dy, *beside, *weights, *after)


def activation_kernel(mine_ref, arrived_ref, after, out, mine, arrived, sems):
    del after
    run_copies([(mine_ref, mine), (arrived_ref, arrived)], sems)
    gate = mine[0] + arrived[0]
    up = mine[1] + arrived[1]
    dh = mine[2] + arrived[2]
    sig = jax.nn.sigmoid(gate)
    active = gate * sig
    slope = sig * (1.0 + gate * (1.0 - sig))
    for i, value in enumerate((dh * up * slope, dh * active, active * up)):
        for chip in range(CHIPS):
            out[chip, i] = value.astype(BF16)


def activation(mine, arrived, after):
    return pl.pallas_call(
        activation_kernel,
        out_shape=jax.ShapeDtypeStruct((CHIPS, 3, ROWS, HID), BF16),
        in_specs=[ANY] * 3,
        out_specs=VMEM,
        scratch_shapes=[
            pltpu.VMEM((3, ROWS, HID), F32),
            pltpu.VMEM((3, ROWS, HID), F32),
            pltpu.SemaphoreType.DMA((2,)),
        ],
        compiler_params=pltpu.CompilerParams(vmem_limit_bytes=VMEM_LIMIT),
        cost_estimate=pl.CostEstimate(flops=20 * ROWS * HID, bytes_accessed=1 << 20, transcendentals=ROWS * HID),
        name="activation",
    )(mine, arrived, after)


def grads_kernel(place, x, dy, beside_x, beside_dy, ahead, back, far_x, far_dy, swapped, *rest):
    acts, (gg, gu, gd, xs, dys, hs, sems) = rest[:2], rest[2:]
    core, chip = place[0], place[2]
    half, own = columns(core * HALF), columns(chip * WIDE + core * HALF)
    here = [(x.at[:, own], dy.at[:, own])]
    here += [
        (a.at[:, half], b.at[:, half])
        for a, b in ((ahead.at[0], ahead.at[1]), (far_x.at[0], far_dy.at[0]), (back.at[0], back.at[1]))
    ]
    there = [(beside_x.at[:, own], beside_dy.at[:, own])]
    there += [(swapped.at[i, 0], swapped.at[i, 1]) for i in range(CHIPS - 1)]
    early, late = [], []
    for i, (a, b) in enumerate(here + there):
        rows = pl.ds(i * ROWS, ROWS)
        source = lax.rem(chip + 2 * CHIPS - i, CHIPS)
        early += [(acts[i // CHIPS].at[source], hs.at[:, rows]), (a, xs.at[rows])]
        late.append((b, dys.at[rows]))
    started = start_copies(early + late, sems)
    tall = (((0,), (0,)), ((), ()))
    wait_copies(started[: len(early)])
    gg[0] = lax.dot_general(xs[...], hs[0], tall, preferred_element_type=F32).astype(BF16)
    gu[0] = lax.dot_general(xs[...], hs[1], tall, preferred_element_type=F32).astype(BF16)
    wait_copies(started[len(early) :])
    gd[0] = lax.dot_general(hs[2], dys[...], tall, preferred_element_type=F32).astype(BF16)


def grads(place, x, dy, beside, arrived, swapped, acts):
    tokens = 2 * CHIPS * ROWS
    return pl.pallas_call(
        grads_kernel,
        out_shape=(
            jax.ShapeDtypeStruct((1, HALF, HID), BF16),
            jax.ShapeDtypeStruct((1, HALF, HID), BF16),
            jax.ShapeDtypeStruct((1, HID, HALF), BF16),
        ),
        in_specs=[SMEM] + [ANY] * (9 + len(acts)),
        out_specs=(VMEM,) * 3,
        scratch_shapes=[
            pltpu.VMEM((tokens, HALF), BF16),
            pltpu.VMEM((tokens, HALF), BF16),
            pltpu.VMEM((3, tokens, HID), BF16),
            pltpu.SemaphoreType.DMA((24,)),
        ],
        compiler_params=pltpu.CompilerParams(vmem_limit_bytes=VMEM_LIMIT),
        cost_estimate=pl.CostEstimate(flops=6 * 1024 * 512 * 256, bytes_accessed=5 << 20, transcendentals=0),
        name="weight_grads",
    )(place, x, dy, *beside, *arrived, swapped, *acts)


def to_shift(value, shift):
    return lax.ppermute(value, "yh", [(i, (i + shift) % CHIPS) for i in range(CHIPS)])


def from_shift(value, shift):
    return lax.ppermute(value, "yh", [(i, (i - shift) % CHIPS) for i in range(CHIPS)])


def from_x(value, shift, size):
    return lax.ppermute(value, "x", [(i, (i - shift) % size) for i in range(size)])


def other_core(value):
    return lax.ppermute(value, "core", [(0, 1), (1, 0)])


def share_of_sum(delta):
    everyone = ("yl", "x", "z")
    count = lax.axis_size(everyone)
    rows, cols = delta.shape
    tiles = delta.reshape(rows // 8, 8, cols // 128, 128).transpose(0, 2, 1, 3).reshape(count, 8, 128)
    return jnp.sum(lax.all_to_all(tiles, everyone, 0, 0, tiled=True), axis=0, keepdims=True)


def whole_mean(part, shape):
    everyone = ("yl", "x", "z")
    count = lax.axis_size(everyone)
    rows, cols = shape
    whole = lax.all_to_all(jnp.broadcast_to(part / count, (count, 8, 128)), everyone, 0, 0, tiled=True)
    return whole.reshape(rows // 8, cols // 128, 8, 128).transpose(0, 2, 1, 3).reshape(rows, cols)


def on_device(tokens, cotangent, w_gate, w_up, w_down, delta, anchor, momentum):
    x, dy = tokens[0], cotangent[0]
    place = jnp.stack([lax.axis_index(name) for name in ("core", "x", "yh")]).astype(jnp.int32)
    parts = lax.axis_size("x")

    share = own_share(place, w_gate, w_up, w_down, parts)
    shares = {shift: from_shift(share, shift) for shift in (1, 2, 3)}
    shares = jnp.stack([share] + [shares[shift] for shift in (1, 2, 3)])
    weights = [shares] + [from_x(shares, shift, parts) for shift in range(1, parts)]

    beside = (other_core(x), other_core(dy))
    part = share_of_sum(staged(delta[0], beside[0]))
    ahead, back = pack(place, x, dy, (shares, *beside))
    ahead, back = to_shift(ahead, 1), to_shift(back, 3)
    far_x, far_dy = onward(ahead, back)
    far_x, far_dy = to_shift(far_x, 1), to_shift(far_dy, 3)
    arrived = [ahead, back, far_x, far_dy]
    repacked = repack(place, arrived)
    swapped = other_core(repacked)

    pseudo = whole_mean(part, anchor.shape)
    new_momentum = 0.9 * momentum + pseudo
    new_anchor = anchor - 0.7 * (pseudo + 0.9 * new_momentum)

    mine, theirs = hidden_sums(place, x, dy, beside, weights, (far_x, far_dy))
    acts = activation(mine, other_core(theirs), new_anchor)
    acts = lax.all_to_all(acts, "yh", 0, 0, tiled=True)
    acts = (acts, other_core(acts))
    grad_gate, grad_up, grad_down = grads(place, x, dy, beside, arrived, swapped, acts)
    return grad_gate, grad_up, grad_down, new_anchor, new_momentum


def solution(mesh):
    fine = Mesh(mesh.devices.reshape(4, 2, 2, 4, 8), ("yh", "core", "yl", "x", "z"))
    fsdp, replica = ("yh", "core"), ("yl", "x", "z")
    placed = (
        P(replica, fsdp, None),
        P(replica, fsdp, None),
        P(fsdp, None),
        P(fsdp, None),
        P(None, fsdp),
        P(replica, fsdp, None),
        P(fsdp, None),
        P(fsdp, None),
    )
    return jax.shard_map(
        on_device,
        mesh=fine,
        in_specs=placed,
        out_specs=(
            P(replica, fsdp, None),
            P(replica, fsdp, None),
            P(replica, None, fsdp),
            P(fsdp, None),
            P(fsdp, None),
        ),
        check_vma=False,
    )
```
